32 devices in a mesh: groups: 2 (over y), trunk: 4 (over z), branch: 2 (over x), tensor: 2 (over core).
Axes of the slice: x: 2, y: 2, z: 4, core: 2. Of those that a mesh axis runs over, the one named last changes fastest.
Arguments:
- query: bfloat16 [4, 128, 4096], P(('groups', 'branch'), 'trunk', 'tensor'), parts along dimension 0, may hold values from -6 to 6
- cotangent: bfloat16 [4, 128, 4096], P(('groups', 'branch'), 'trunk', 'tensor'), parts along dimension 0, may hold values from -6 to 6
- branch_keys: bfloat16 [4, 128, 512], P(('groups', 'branch'), 'trunk', 'tensor'), parts along dimension 0, may hold values from -6 to 6
- rollout_value_rows: bfloat16 [4, 128, 512], P(('groups', 'branch'), 'trunk', 'tensor'), parts along dimension 0, may hold values from -6 to 6
- trunk_keys: bfloat16 [2048, 512], P(('groups', 'trunk', 'branch'), 'tensor'), parts along dimension 0, may hold values from -6 to 6
- shared_trunk_values: bfloat16 [2048, 512], P(('groups', 'trunk', 'branch'), 'tensor'), parts along dimension 0, may hold values from -6 to 6
- forks: int32 [4], P(('groups', 'branch')), parts along dimension 0, may hold values from 2 to 1024, as said below
- lengths: int32 [4], P(('groups', 'branch')), parts along dimension 0, may hold values from 32 to 128, as said below
Outputs:
- query_grad: bfloat16 [4, 128, 4096], P(('groups', 'branch'), 'trunk', 'tensor'), parts along dimension 0
- trunk_key_grad: bfloat16 [2048, 512], P(('groups', 'trunk', 'branch'), 'tensor'), parts along dimension 0
- trunk_value_grad: bfloat16 [2048, 512], P(('groups', 'trunk', 'branch'), 'tensor'), parts along dimension 0
- branch_key_grad: bfloat16 [4, 128, 512], P(('groups', 'branch'), 'trunk', 'tensor'), parts along dimension 0
- branch_value_grad: bfloat16 [4, 128, 512], P(('groups', 'branch'), 'trunk', 'tensor'), parts along dimension 0
The draws below stay inside these ranges and needn't reach their ends.
There are 2 independent parts, one for each index of `groups`. The reference program is written for one: setup_inputs(seed, part) draws one part's arguments, and reference() takes and returns one part's arrays. A program takes and returns all parts, laid end to end along the dimension named above; each array names one. Nothing has to cross between parts.
Inputs may be any that keep to these rules, and one draw needn't show every extreme that they name: Some rollout forks at the end of the trunk in every draw. `lengths`: some rollout fills all 128 positions in every draw.
All inputs are finite; a program needn't handle non-finite values.
Results may differ from the reference program's by a relative error of at most 0.028.
Values may be sent and summed in bfloat16 or wider, within the bound.
A program may use at most 64 MiB of HBM per device.

```python
import jax
import jax.numpy as jnp
from jax import lax

QUERY_HEADS = 32
KEY_VALUE_HEADS = 4
HEAD_WIDTH = 128
ROLLOUT_LENGTH = 128
TRUNK_LENGTH = 1024
ROLLOUT_COUNT = 2


def trunk_sign_draws(key):
    sign_bits = jax.random.randint(jax.random.fold_in(key, 101), (KEY_VALUE_HEADS, HEAD_WIDTH), 0, 2)
    return (2 * sign_bits - 1).astype(jnp.float32)


def rollout_sign_draws(key):
    sign_bits = jax.random.randint(jax.random.fold_in(key, 102), (ROLLOUT_COUNT, KEY_VALUE_HEADS, HEAD_WIDTH), 0, 2)
    return (2 * sign_bits - 1).astype(jnp.float32)


def paired_rows(random_signs):
    shorter = jnp.arange(HEAD_WIDTH) < max(1, HEAD_WIDTH // 16)
    leading = 5.0 * random_signs
    second = random_signs * jnp.where(shorter, 4.5, 5.0)
    flattened_shape = random_signs.shape[:-2] + (KEY_VALUE_HEADS * HEAD_WIDTH,)
    return (leading.reshape(flattened_shape), second.reshape(flattened_shape))


def draw_forks(key, part):
    key = jax.random.fold_in(key, 11)
    first, second = jax.random.split(key)
    values = jax.random.randint(first, (ROLLOUT_COUNT,), 2, TRUNK_LENGTH + 1)
    chosen = jax.random.randint(second, (), 0, ROLLOUT_COUNT)
    return values.at[chosen].set(TRUNK_LENGTH).astype(jnp.int32)


def draw_lengths(key, part):
    key = jax.random.fold_in(key, 23)
    first, second = jax.random.split(key)
    values = jax.random.randint(first, (ROLLOUT_COUNT,), ROLLOUT_LENGTH // 4, ROLLOUT_LENGTH + 1)
    chosen = jax.random.randint(second, (), 0, ROLLOUT_COUNT)
    return values.at[chosen].set(ROLLOUT_LENGTH).astype(jnp.int32)


def draw_trunk_keys(key, part):
    random_signs = trunk_sign_draws(key)
    key = jax.random.fold_in(key, 31)
    first = jax.random.fold_in(key, 0)
    tensor_shape = (TRUNK_LENGTH, KEY_VALUE_HEADS * HEAD_WIDTH)
    values = jnp.clip(jax.random.normal(first, tensor_shape, jnp.float32), -6.0, 6.0)
    leading, following = paired_rows(random_signs)
    values = values.at[0].set(leading).at[1].set(following)
    return values.astype(jnp.bfloat16)


def draw_branch_keys(key, part):
    random_signs = rollout_sign_draws(key)
    key = jax.random.fold_in(key, 37)
    first = jax.random.fold_in(key, 0)
    tensor_shape = (ROLLOUT_COUNT, ROLLOUT_LENGTH, KEY_VALUE_HEADS * HEAD_WIDTH)
    values = jnp.clip(jax.random.normal(first, tensor_shape, jnp.float32), -6.0, 6.0)
    leading, following = paired_rows(random_signs)
    values = values.at[:, 0].set(leading).at[:, 1].set(following)
    return values.astype(jnp.bfloat16)


def draw_query(key, part):
    trunk_directions = jnp.repeat(trunk_sign_draws(key), QUERY_HEADS // KEY_VALUE_HEADS, axis=0)
    rollout_directions = jnp.repeat(rollout_sign_draws(key), QUERY_HEADS // KEY_VALUE_HEADS, axis=1)
    key = jax.random.fold_in(key, 41)
    first = jax.random.fold_in(key, 0)
    third = jax.random.fold_in(key, 2)
    fourth = jax.random.fold_in(key, 3)
    tensor_shape = (ROLLOUT_COUNT, ROLLOUT_LENGTH, QUERY_HEADS, HEAD_WIDTH)
    values = jnp.clip(jax.random.normal(first, tensor_shape, jnp.float32), -6.0, 6.0)
    picks = jax.random.randint(third, (ROLLOUT_COUNT, ROLLOUT_LENGTH, QUERY_HEADS), 0, 50)
    levels = jax.random.randint(fourth, (ROLLOUT_COUNT, ROLLOUT_LENGTH, QUERY_HEADS), 0, 3)
    strength = jnp.array([3.0, 4.0, 6.0], jnp.float32)[levels]
    rows = jnp.arange(ROLLOUT_LENGTH)
    live = ((rows >= 2) & (rows < ROLLOUT_LENGTH // 4))[None, :, None]
    aligned_trunk = strength[..., None] * trunk_directions[None, None]
    aligned_own = strength[..., None] * rollout_directions[:, None]
    values = jnp.where(((picks == 0) & live)[..., None], aligned_trunk, values)
    values = jnp.where(((picks == 1) & live)[..., None], aligned_own, values)
    return values.reshape(ROLLOUT_COUNT, ROLLOUT_LENGTH, QUERY_HEADS * HEAD_WIDTH).astype(jnp.bfloat16)


def block_levels(rng, shape, cuts, low, top_value):
    gain, own = 1.0, jax.random.fold_in(rng, 6)
    for axis_at, shards_of in cuts:
        draws = jnp.exp(jax.random.uniform(jax.random.fold_in(own, axis_at), (shards_of,), jnp.float32, low / len(cuts), top_value / len(cuts)))
        gain = gain * jnp.repeat(draws, shape[axis_at] // shards_of).reshape([-1 if axis == axis_at else 1 for axis in range(len(shape))])
    return gain


def gaussian(key, extent, spread, limit, cuts=(), kind=jnp.bfloat16):
    values = spread * jax.random.normal(key, extent, jnp.float32)
    if cuts:
        values = values * block_levels(key, extent, cuts, -0.22, 0.18)
    return jnp.clip(values, -limit, limit).astype(kind)


def setup_inputs(seed: int = 0, part: int = 0) -> dict:
    arg_keys = jax.random.split(jax.random.key(seed), 9)
    part_splits = jax.random.split(jax.random.fold_in(arg_keys[8], part), 9)
    query = draw_query(jax.random.fold_in(jax.random.fold_in(arg_keys[8], part), 71), part)
    cotangent = gaussian(part_splits[1], (ROLLOUT_COUNT, ROLLOUT_LENGTH, QUERY_HEADS * HEAD_WIDTH), 1.0, 6.0, ((0, 2), (1, 4), (2, 2)))
    branch_keys = draw_branch_keys(jax.random.fold_in(jax.random.fold_in(arg_keys[8], part), 71), part)
    rollout_value_rows = gaussian(part_splits[3], (ROLLOUT_COUNT, ROLLOUT_LENGTH, KEY_VALUE_HEADS * HEAD_WIDTH), 1.0, 6.0, ((0, 2), (1, 4), (2, 2)))
    trunk_keys = draw_trunk_keys(jax.random.fold_in(jax.random.fold_in(arg_keys[8], part), 71), part)
    shared_trunk_values = gaussian(part_splits[5], (TRUNK_LENGTH, KEY_VALUE_HEADS * HEAD_WIDTH), 1.0, 6.0, ((0, 8), (1, 2)))
    forks = draw_forks(jax.random.fold_in(jax.random.fold_in(arg_keys[8], part), 71), part)
    lengths = draw_lengths(jax.random.fold_in(jax.random.fold_in(arg_keys[8], part), 71), part)
    return {"query": query, "cotangent": cotangent, "branch_keys": branch_keys, "rollout_value_rows": rollout_value_rows, "trunk_keys": trunk_keys, "shared_trunk_values": shared_trunk_values, "forks": forks, "lengths": lengths}


def reference(query, cotangent, branch_keys, rollout_value_rows, trunk_keys, shared_trunk_values, forks, lengths):
    scale_factor = HEAD_WIDTH ** -0.5
    group_rollouts = QUERY_HEADS // KEY_VALUE_HEADS
    positions = jnp.arange(ROLLOUT_LENGTH, dtype=jnp.int32)
    trunk_positions = jnp.arange(TRUNK_LENGTH, dtype=jnp.int32)

    def one_rollout(carry, inputs):
        query_vectors, output_gradients, own_keys, own_values, fork_point, length = inputs
        is_valid = positions < length
        output_gradients = output_gradients * is_valid[:, None].astype(jnp.bfloat16)
        combined_keys = jnp.concatenate([trunk_keys, own_keys], 0)
        combined_values = jnp.concatenate([shared_trunk_values, own_values], 0)
        trunk_seen = jnp.broadcast_to(trunk_positions[None, :] < fork_point, (ROLLOUT_LENGTH, TRUNK_LENGTH))
        own_seen = (positions[None, :] <= positions[:, None]) & (positions[None, :] < length)
        visible = jnp.concatenate([trunk_seen, own_seen], 1)
        head_queries = query_vectors.reshape(ROLLOUT_LENGTH, KEY_VALUE_HEADS, group_rollouts, HEAD_WIDTH).transpose(1, 2, 0, 3)
        gradient_heads = output_gradients.reshape(ROLLOUT_LENGTH, KEY_VALUE_HEADS, group_rollouts, HEAD_WIDTH).transpose(1, 2, 0, 3)
        head_keys = combined_keys.reshape(-1, KEY_VALUE_HEADS, HEAD_WIDTH).transpose(1, 0, 2)
        head_values = combined_values.reshape(-1, KEY_VALUE_HEADS, HEAD_WIDTH).transpose(1, 0, 2)

        def one_group(items):
            query_one, grad_one, key_one, value_one = items
            scores = jnp.einsum("hsd,kd->hsk", query_one.astype(jnp.float32), key_one.astype(jnp.float32)) * scale_factor
            scores = jnp.where(visible[None], scores, -1e30)
            row_max = jnp.max(scores, -1, keepdims=True)
            weights = jnp.exp(scores - row_max)
            probs = weights / jnp.sum(weights, -1, keepdims=True)
            dprobs = jnp.einsum("hsd,kd->hsk", grad_one.astype(jnp.float32), value_one.astype(jnp.float32))
            delta = jnp.sum(probs * dprobs, -1, keepdims=True)
            probs_low = probs.astype(jnp.bfloat16).astype(jnp.float32)
            dscores = (probs * (dprobs - delta) * scale_factor).astype(jnp.bfloat16).astype(jnp.float32)
            dquery = jnp.einsum("hsk,kd->hsd", dscores, key_one.astype(jnp.float32))
            key_gradient = jnp.einsum("hsk,hsd->kd", dscores, query_one.astype(jnp.float32))
            value_gradient = jnp.einsum("hsk,hsd->kd", probs_low, grad_one.astype(jnp.float32))
            return dquery, key_gradient, value_gradient

        dquery, key_gradient, value_gradient = lax.map(one_group, (head_queries, gradient_heads, head_keys, head_values))
        dquery = dquery.transpose(2, 0, 1, 3).reshape(ROLLOUT_LENGTH, QUERY_HEADS * HEAD_WIDTH)
        key_gradient = key_gradient.transpose(1, 0, 2).reshape(-1, KEY_VALUE_HEADS * HEAD_WIDTH)
        value_gradient = value_gradient.transpose(1, 0, 2).reshape(-1, KEY_VALUE_HEADS * HEAD_WIDTH)
        carry = (carry[0] + key_gradient[:TRUNK_LENGTH], carry[1] + value_gradient[:TRUNK_LENGTH])
        outputs = (dquery.astype(jnp.bfloat16), key_gradient[TRUNK_LENGTH:].astype(jnp.bfloat16), value_gradient[TRUNK_LENGTH:].astype(jnp.bfloat16))
        return carry, outputs

    zero_filled = jnp.zeros((TRUNK_LENGTH, KEY_VALUE_HEADS * HEAD_WIDTH), jnp.float32)
    totals, outputs = lax.scan(one_rollout, (zero_filled, zero_filled), (query, cotangent, branch_keys, rollout_value_rows, forks, lengths))
    return (outputs[0], totals[0].astype(jnp.bfloat16), totals[1].astype(jnp.bfloat16), outputs[1], outputs[2])
```

```python
import jax
import jax.numpy as jnp
from jax import lax
from jax.experimental import pallas as pl
from jax.experimental.pallas import tpu as pltpu
from jax.sharding import PartitionSpec as P

HEAD_WIDTH = 128


def shards(
    query,
    cotangent,
    branch_keys,
    rollout_value_rows,
    trunk_keys,
    shared_trunk_values,
    forks,
    lengths,
):
    scale_factor = HEAD_WIDTH ** (-0.5)
    query_vectors, output_gradients = (
        lax.all_gather(query, "trunk", axis=1, tiled=True),
        lax.all_gather(cotangent, "trunk", axis=1, tiled=True),
    )
    slab_keys, slab_values = (
        lax.all_gather(trunk_keys, "branch", axis=0, tiled=True),
        lax.all_gather(shared_trunk_values, "branch", axis=0, tiled=True),
    )
    trunk_index = lax.axis_index("trunk")
    slab_rows = slab_keys.shape[0]
    block_rows = branch_keys.shape[1]
    seq_rows = query_vectors.shape[1]
    fork_point = forks[0]
    length = lengths[0]
    positions = jnp.arange(seq_rows, dtype=jnp.int32)
    is_valid = positions < length
    output_gradients = output_gradients[0] * is_valid[:, None].astype(jnp.bfloat16)
    keys_local = jnp.concatenate([slab_keys, branch_keys[0]], 0)
    values_local = jnp.concatenate([slab_values, rollout_value_rows[0]], 0)
    slab_positions = trunk_index * slab_rows + jnp.arange(slab_rows, dtype=jnp.int32)
    block_positions = trunk_index * block_rows + jnp.arange(block_rows, dtype=jnp.int32)
    trunk_seen = jnp.broadcast_to(slab_positions[None, :] < fork_point, (seq_rows, slab_rows))
    own_seen = (block_positions[None, :] <= positions[:, None]) & (
        block_positions[None, :] < length
    )
    visible = jnp.concatenate([trunk_seen, own_seen], 1)
    kv_heads = keys_local.shape[1] // HEAD_WIDTH
    q_heads = query_vectors.shape[2] // HEAD_WIDTH
    group_rollouts = q_heads // kv_heads
    head_queries = (
        query_vectors[0]
        .reshape(seq_rows, kv_heads, group_rollouts, HEAD_WIDTH)
        .transpose(1, 2, 0, 3)
    )
    gradient_heads = output_gradients.reshape(
        seq_rows, kv_heads, group_rollouts, HEAD_WIDTH
    ).transpose(1, 2, 0, 3)
    head_keys = keys_local.reshape(-1, kv_heads, HEAD_WIDTH).transpose(1, 0, 2)
    head_values = values_local.reshape(-1, kv_heads, HEAD_WIDTH).transpose(1, 0, 2)

    def scores_of(query_one, key_one):
        scores = (
            jnp.einsum("hsd,kd->hsk", query_one, key_one, preferred_element_type=jnp.float32)
            * scale_factor
        )
        return jnp.where(visible[None], scores, -1e30)

    def local_max(items):
        return jnp.max(scores_of(items[0], items[1]), -1)

    row_max = lax.pmax(lax.map(local_max, (head_queries, head_keys)), "trunk")

    def local_total(items):
        return jnp.sum(jnp.exp(scores_of(items[0], items[1]) - items[2][..., None]), -1)

    row_total = lax.psum(lax.map(local_total, (head_queries, head_keys, row_max)), "trunk")

    def probs_of(query_one, key_one, largest, total):
        return jnp.exp(scores_of(query_one, key_one) - largest[..., None]) / total[..., None]

    def local_delta(items):
        query_one, grad_one, key_one, value_one, largest, total = items
        probs = probs_of(query_one, key_one, largest, total)
        dprobs = jnp.einsum("hsd,kd->hsk", grad_one, value_one, preferred_element_type=jnp.float32)
        return jnp.sum(probs * dprobs, -1)

    stacked = (head_queries, gradient_heads, head_keys, head_values, row_max, row_total)
    delta = lax.psum(lax.map(local_delta, stacked), "trunk")

    def grads_of(items):
        query_one, grad_one, key_one, value_one, largest, total, delta_one = items
        probs = probs_of(query_one, key_one, largest, total)
        dprobs = jnp.einsum("hsd,kd->hsk", grad_one, value_one, preferred_element_type=jnp.float32)
        probs_low = probs.astype(jnp.bfloat16)
        dscores = (probs * (dprobs - delta_one[..., None]) * scale_factor).astype(jnp.bfloat16)
        key_gradient = jnp.einsum(
            "hsk,hsd->kd", dscores, query_one, preferred_element_type=jnp.float32
        )
        value_gradient = jnp.einsum(
            "hsk,hsd->kd", probs_low, grad_one, preferred_element_type=jnp.float32
        )
        return (dscores, key_gradient, value_gradient)

    def local_grads(items):
        dscores, key_gradient, value_gradient = grads_of(items)
        dquery = jnp.einsum("hsk,kd->hsd", dscores, items[2], preferred_element_type=jnp.float32)
        return (dquery, key_gradient, value_gradient)

    dquery, key_gradient, value_gradient = lax.map(local_grads, stacked + (delta,))
    dquery = dquery.transpose(2, 0, 1, 3).reshape(1, seq_rows, q_heads * HEAD_WIDTH)
    query_grad = lax.psum_scatter(
        dquery.astype(jnp.bfloat16), "trunk", scatter_dimension=1, tiled=True
    )
    key_gradient = key_gradient.transpose(1, 0, 2).reshape(-1, kv_heads * HEAD_WIDTH)
    value_gradient = value_gradient.transpose(1, 0, 2).reshape(-1, kv_heads * HEAD_WIDTH)
    trunk_key_grad, trunk_value_grad = (
        lax.psum_scatter(
            key_gradient[:slab_rows].astype(jnp.bfloat16), "branch", scatter_dimension=0, tiled=True
        ).astype(jnp.float32),
        lax.psum_scatter(
            value_gradient[:slab_rows].astype(jnp.bfloat16),
            "branch",
            scatter_dimension=0,
            tiled=True,
        ).astype(jnp.float32),
    )
    branch_key_grad = key_gradient[slab_rows:][None].astype(jnp.bfloat16)
    branch_value_grad = value_gradient[slab_rows:][None].astype(jnp.bfloat16)
    return (
        query_grad,
        trunk_key_grad.astype(jnp.bfloat16),
        trunk_value_grad.astype(jnp.bfloat16),
        branch_key_grad,
        branch_value_grad,
    )


MESH = pl.DeviceIdType.MESH
W = HEAD_WIDTH
NT = (((1,), (1,)), ((), ()))
TN = (((0,), (0,)), ((), ()))
HIDDEN = -1e30


def dot(lhs, rhs, dims=None):
    if dims is None:
        return jnp.dot(lhs, rhs, preferred_element_type=jnp.float32)
    return lax.dot_general(lhs, rhs, dims, preferred_element_type=jnp.float32)


def fused_kernel(
    forks,
    lengths,
    query,
    cotangent,
    branch_keys,
    branch_values,
    trunk_keys,
    trunk_values,
    query_grad,
    trunk_key_grad,
    trunk_value_grad,
    branch_key_grad,
    branch_value_grad,
    q_in,
    c_in,
    kv,
    own,
    q_rows,
    c_rows,
    scores,
    dprobs,
    dq_total,
    mine,
    x_out,
    x_in,
    z_out,
    z_in,
    own_out,
    own_in,
    dq_out,
    local_sem,
    z_send,
    z_recv,
    x_send,
    x_recv,
    back_send,
    back_recv,
):
    z = lax.axis_index("trunk")
    x = lax.axis_index("branch")
    head = lax.rem(z, 2)
    at = (z, z + 1 - 2 * head, lax.rem(z + 2, 4), 3 - z)
    other_x = {"branch": 1 - x}
    rows = query.shape[1]
    slab = trunk_keys.shape[0]
    group = query.shape[2] // 2 // W
    wide = group * W
    cols = 2 * group * rows
    scale = W ** (-0.5)

    def head_cols(index, width):
        return pl.ds(pl.multiple_of(index * width, width), width)

    barrier = pltpu.get_barrier_semaphore()
    for d in (1, 2, 3):
        pl.semaphore_signal(barrier, inc=1, device_id={"trunk": at[d]}, device_id_type=MESH)
    pl.semaphore_signal(barrier, inc=1, device_id=other_x, device_id_type=MESH)
    pl.semaphore_wait(barrier, 4)

    def remote(src, dst, send, recv, device):
        return pltpu.make_async_remote_copy(
            src_ref=src,
            dst_ref=dst,
            send_sem=send,
            recv_sem=recv,
            device_id=device,
            device_id_type=MESH,
        )

    mine_cols = head_cols(head, W)
    x_copies = {}
    first = []
    for n, ref in enumerate((trunk_keys, trunk_values)):
        first.append(
            remote(
                ref.at[:, mine_cols], kv.at[1, 0, n], x_send.at[0, n], x_recv.at[0, n], other_x
            )
        )
    x_copies[0] = first
    z_copies = {}
    for d in (1, 2, 3):
        sent = head_cols(lax.rem(at[d], 2), W)
        to = {"trunk": at[d]}
        z_copies[d] = [
            remote(ref.at[:, sent], kv.at[0, d, n], z_send.at[d, n], z_recv.at[d, n], to)
            for n, ref in enumerate((trunk_keys, trunk_values))
        ] + [
            remote(ref.at[0, :, sent], own.at[n, d], z_send.at[d, 2 + n], z_recv.at[d, 2 + n], to)
            for n, ref in enumerate((branch_keys, branch_values))
        ]
    pair_cols = head_cols(1 - head, wide)
    q_copies = [
        remote(
            ref.at[0, :, pair_cols], dst.at[1], z_send.at[0, n], z_recv.at[0, n], {"trunk": at[1]}
        )
        for n, (ref, dst) in enumerate(((query, q_in), (cotangent, c_in)))
    ]
    for copy in z_copies[1][:2] + x_copies[0] + z_copies[2][:2] + z_copies[3][:2]:
        copy.start()
    for copy in q_copies:
        copy.start()
    for d in (1, 2, 3):
        for copy in z_copies[d][2:]:
            copy.start()
    local = []
    for n, ref in enumerate((trunk_keys, trunk_values)):
        local.append(pltpu.make_async_copy(ref.at[:, mine_cols], kv.at[0, 0, n], local_sem.at[n]))
    for n, ref in enumerate((branch_keys, branch_values)):
        local.append(
            pltpu.make_async_copy(ref.at[0, :, mine_cols], own.at[n, 0], local_sem.at[2 + n])
        )
    for n, (ref, dst) in enumerate(((query, q_in), (cotangent, c_in))):
        local.append(
            pltpu.make_async_copy(
                ref.at[0, :, head_cols(head, wide)], dst.at[0], local_sem.at[4 + n]
            )
        )
    for copy in local:
        copy.start()

    for d in (1, 2, 3):
        for copy in z_copies[d][:2]:
            copy.wait_recv()
        x_copies[d] = [
            remote(kv.at[0, d], kv.at[1, d], x_send.at[d, 0], x_recv.at[d, 0], other_x)
        ]
        x_copies[d][0].start()
    for copy in local:
        copy.wait()
    for copy in q_copies:
        copy.wait_recv()

    fork = forks[0]
    length = lengths[0]
    row_iota = lax.broadcasted_iota(jnp.int32, (rows, W), 0)
    for e in (0, 1):
        live = (row_iota + at[e] * rows < length).astype(jnp.float32)
        for g in range(group):
            start = (e * group + g) * rows
            q_rows[start : start + rows, :] = q_in[e, :, g * W : (g + 1) * W]
            part = c_in[e, :, g * W : (g + 1) * W].astype(jnp.float32) * live
            c_rows[start : start + rows, :] = part.astype(jnp.bfloat16)

    col = lax.broadcasted_iota(jnp.int32, (1, cols), 1)
    half = group * rows
    col_pos = jnp.where(col < half, at[0], at[1]) * rows + lax.rem(col, rows)
    slab_iota = lax.broadcasted_iota(jnp.int32, (slab, 1), 0)

    blocks = [(r, d) for r in (0, 1) for d in range(4)]
    base_of = {block: i * slab for i, block in enumerate(blocks)}
    own_base = len(blocks) * slab
    own_rows = 4 * rows

    def score(base, size, key, value, seen):
        part = dot(key, q_rows[...], NT) * scale
        part = jnp.where(seen, part, HIDDEN)
        scores[base : base + size, :] = part
        dprobs[base : base + size, :] = dot(value, c_rows[...], NT)
        return jnp.max(part, 0, keepdims=True)

    def trunk_score(r, d):
        side = x if r == 0 else 1 - x
        seen = slab_iota + (at[d] * 2 + side) * slab < fork
        return score(base_of[r, d], slab, kv[r, d, 0], kv[r, d, 1], seen)

    largest = trunk_score(0, 0)
    for d in (1, 2, 3):
        largest = jnp.maximum(largest, trunk_score(0, d))
    for d in (1, 2, 3):
        for copy in z_copies[d][2:]:
            copy.wait_recv()
    own_iota = lax.broadcasted_iota(jnp.int32, (rows, 1), 0)
    own_pos = jnp.concatenate([own_iota + at[d] * rows for d in range(4)], 0)
    own_key = own[0].reshape(own_rows, W)
    own_value = own[1].reshape(own_rows, W)
    largest = jnp.maximum(
        largest,
        score(
            own_base, own_rows, own_key, own_value, (own_pos <= col_pos) & (own_pos < length)
        ),
    )
    for d in range(4):
        for copy in x_copies[d]:
            copy.wait_recv()
        largest = jnp.maximum(largest, trunk_score(1, d))

    total = jnp.zeros((1, cols), jnp.float32)
    delta = jnp.zeros((1, cols), jnp.float32)
    for base in range(0, own_base + own_rows, W):
        weights = jnp.exp(scores[base : base + W, :] - largest)
        scores[base : base + W, :] = weights
        total += jnp.sum(weights, 0, keepdims=True)
        delta += jnp.sum(weights * dprobs[base : base + W, :], 0, keepdims=True)
    inverse = 1.0 / total
    delta = delta * inverse
    dq_total[...] = jnp.zeros_like(dq_total)

    def grads(base, size, key):
        probs = scores[base : base + size, :] * inverse
        low = probs.astype(jnp.bfloat16)
        dscores = (probs * (dprobs[base : base + size, :] - delta) * scale).astype(jnp.bfloat16)
        dq_total[...] += dot(key, dscores, TN)
        return dot(dscores, q_rows[...]), dot(low, c_rows[...])

    back = {}
    for d in (3, 2, 1, 0):
        pair = grads(base_of[1, d], slab, kv[1, d, 0])
        for n in (0, 1):
            x_out[d, n] = pair[n].astype(jnp.bfloat16)
        back[d] = remote(x_out.at[d], x_in.at[d], back_send.at[d], back_recv.at[d], other_x)
        back[d].start()
    pair = grads(own_base, own_rows, own_key)
    for n in (0, 1):
        mine_part = pair[n].astype(jnp.bfloat16)
        for d in range(4):
            own_out[d, n] = mine_part[d * rows : (d + 1) * rows, :]
    for d in (3, 2, 1):
        back[4 + d] = remote(
            own_out.at[d],
            own_in.at[d],
            back_send.at[4 + d],
            back_recv.at[4 + d],
            {"trunk": at[d]},
        )
        back[4 + d].start()
    for d in (3, 2, 1, 0):
        pair = grads(base_of[0, d], slab, kv[0, d, 0])
        for n in (0, 1):
            mine[d, n] = pair[n]
    for d in (3, 2):
        back[d].wait_recv()
        z_out[d] = (mine[d] + x_in[d].astype(jnp.float32)).astype(jnp.bfloat16)
        back[8 + d] = remote(
            z_out.at[d], z_in.at[d], back_send.at[8 + d], back_recv.at[8 + d], {"trunk": at[d]}
        )
        back[8 + d].start()
    dq = dq_total[...].T.astype(jnp.bfloat16)
    for g in range(group):
        dq_out[:, g * W : (g + 1) * W] = dq[half + g * rows : half + (g + 1) * rows, :]
    back[4] = remote(
        dq_out,
        query_grad.at[0, :, head_cols(head, wide)],
        back_send.at[4],
        back_recv.at[4],
        {"trunk": at[1]},
    )
    back[4].start()
    back[1].wait_recv()
    z_out[1] = (mine[1] + x_in[1].astype(jnp.float32)).astype(jnp.bfloat16)
    back[9] = remote(
        z_out.at[1], z_in.at[1], back_send.at[9], back_recv.at[9], {"trunk": at[1]}
    )
    back[9].start()
    for g in range(group):
        query_grad[0, :, pl.ds(pl.multiple_of(head * wide + g * W, W), W)] = dq[
            g * rows : (g + 1) * rows, :
        ]
    back[0].wait_recv()
    kept = mine[0] + x_in[0].astype(jnp.float32)
    f32 = jnp.float32
    theirs = head_cols(1 - head, W)
    for d in (3, 2, 1):
        back[4 + d].wait_recv()
    for n, ref in enumerate((branch_key_grad, branch_value_grad)):
        ref[0, :, mine_cols] = (own_out[0, n].astype(f32) + own_in[2, n].astype(f32)).astype(
            jnp.bfloat16
        )
        ref[0, :, theirs] = (own_in[1, n].astype(f32) + own_in[3, n].astype(f32)).astype(
            jnp.bfloat16
        )
    back[10].wait_recv()
    for n, ref in enumerate((trunk_key_grad, trunk_value_grad)):
        ref[:, mine_cols] = (kept[n] + z_in[2, n].astype(f32)).astype(jnp.bfloat16)
    back[11].wait_recv()
    back[9].wait_recv()
    for n, ref in enumerate((trunk_key_grad, trunk_value_grad)):
        ref[:, theirs] = (z_in[1, n].astype(f32) + z_in[3, n].astype(f32)).astype(jnp.bfloat16)
    back[4].wait_recv()
    for copy in q_copies + sum(z_copies.values(), []) + sum(x_copies.values(), []):
        copy.wait_send()
    for copy in back.values():
        copy.wait_send()


def fused(
    query,
    cotangent,
    branch_keys,
    rollout_value_rows,
    trunk_keys,
    shared_trunk_values,
    forks,
    lengths,
):
    rows = query.shape[1]
    slab = trunk_keys.shape[0]
    wide = query.shape[2] // 2
    cols = 2 * rows * (wide // W)
    keys = 8 * slab + 4 * rows
    bf16, f32 = jnp.bfloat16, jnp.float32
    smem = pl.BlockSpec(memory_space=pltpu.SMEM)
    anywhere = pl.BlockSpec(memory_space=pl.ANY)
    vmem = pl.BlockSpec(memory_space=pltpu.VMEM)

    def like(a):
        return jax.ShapeDtypeStruct(a.shape, a.dtype)

    dma = pltpu.SemaphoreType.DMA
    return pl.pallas_call(
        fused_kernel,
        out_shape=(
            like(query),
            like(trunk_keys),
            like(shared_trunk_values),
            like(branch_keys),
            like(rollout_value_rows),
        ),
        in_specs=[smem] * 2 + [anywhere] * 6,
        out_specs=(vmem,) * 5,
        scratch_shapes=[
            pltpu.VMEM((2, rows, wide), bf16),
            pltpu.VMEM((2, rows, wide), bf16),
            pltpu.VMEM((2, 4, 2, slab, W), bf16),
            pltpu.VMEM((2, 4, rows, W), bf16),
            pltpu.VMEM((cols, W), bf16),
            pltpu.VMEM((cols, W), bf16),
            pltpu.VMEM((keys, cols), f32),
            pltpu.VMEM((keys, cols), f32),
            pltpu.VMEM((W, cols), f32),
            pltpu.VMEM((4, 2, slab, W), f32),
            pltpu.VMEM((4, 2, slab, W), bf16),
            pltpu.VMEM((4, 2, slab, W), bf16),
            pltpu.VMEM((4, 2, slab, W), bf16),
            pltpu.VMEM((4, 2, slab, W), bf16),
            pltpu.VMEM((4, 2, rows, W), bf16),
            pltpu.VMEM((4, 2, rows, W), bf16),
            pltpu.VMEM((rows, wide), bf16),
            dma((6,)),
            dma((4, 4)),
            dma((4, 4)),
            dma((4, 2)),
            dma((4, 2)),
            dma((12,)),
            dma((12,)),
        ],
        compiler_params=pltpu.CompilerParams(
            collective_id=0, has_side_effects=True, vmem_limit_bytes=32 * 1024 * 1024
        ),
        cost_estimate=pl.CostEstimate(
            flops=10 * keys * cols * W, bytes_accessed=2**20, transcendentals=keys * cols
        ),
    )(
        forks,
        lengths,
        query,
        cotangent,
        branch_keys,
        rollout_value_rows,
        trunk_keys,
        shared_trunk_values,
    )


def plan_of(mesh):
    if mesh.shape["trunk"] == 4 and mesh.shape["branch"] == 2:
        return fused
    return shards


def solution(mesh):
    return jax.shard_map(
        plan_of(mesh),
        mesh=mesh,
        in_specs=(
            P(("groups", "branch"), "trunk", "tensor"),
            P(("groups", "branch"), "trunk", "tensor"),
            P(("groups", "branch"), "trunk", "tensor"),
            P(("groups", "branch"), "trunk", "tensor"),
            P(("groups", "trunk", "branch"), "tensor"),
            P(("groups", "trunk", "branch"), "tensor"),
            P(("groups", "branch")),
            P(("groups", "branch")),
        ),
        out_specs=(
            P(("groups", "branch"), "trunk", "tensor"),
            P(("groups", "trunk", "branch"), "tensor"),
            P(("groups", "trunk", "branch"), "tensor"),
            P(("groups", "branch"), "trunk", "tensor"),
            P(("groups", "branch"), "trunk", "tensor"),
        ),
        check_vma=False,
    )
```

```python
import jax
import jax.numpy as jnp
from jax import lax
from jax.experimental import pallas as pl
from jax.experimental.pallas import tpu as pltpu
from jax.sharding import PartitionSpec as P

HEAD_WIDTH = 128


def shards(
    query,
    cotangent,
    branch_keys,
    rollout_value_rows,
    trunk_keys,
    shared_trunk_values,
    forks,
    lengths,
):
    scale_factor = HEAD_WIDTH ** (-0.5)
    query_vectors, output_gradients = (
        lax.all_gather(query, "trunk", axis=1, tiled=True),
        lax.all_gather(cotangent, "trunk", axis=1, tiled=True),
    )
    slab_keys, slab_values = (
        lax.all_gather(trunk_keys, "branch", axis=0, tiled=True),
        lax.all_gather(shared_trunk_values, "branch", axis=0, tiled=True),
    )
    trunk_index = lax.axis_index("trunk")
    slab_rows = slab_keys.shape[0]
    block_rows = branch_keys.shape[1]
    seq_rows = query_vectors.shape[1]
    fork_point = forks[0]
    length = lengths[0]
    positions = jnp.arange(seq_rows, dtype=jnp.int32)
    is_valid = positions < length
    output_gradients = output_gradients[0] * is_valid[:, None].astype(jnp.bfloat16)
    keys_local = jnp.concatenate([slab_keys, branch_keys[0]], 0)
    values_local = jnp.concatenate([slab_values, rollout_value_rows[0]], 0)
    slab_positions = trunk_index * slab_rows + jnp.arange(slab_rows, dtype=jnp.int32)
    block_positions = trunk_index * block_rows + jnp.arange(block_rows, dtype=jnp.int32)
    trunk_seen = jnp.broadcast_to(slab_positions[None, :] < fork_point, (seq_rows, slab_rows))
    own_seen = (block_positions[None, :] <= positions[:, None]) & (
        block_positions[None, :] < length
    )
    visible = jnp.concatenate([trunk_seen, own_seen], 1)
    kv_heads = keys_local.shape[1] // HEAD_WIDTH
    q_heads = query_vectors.shape[2] // HEAD_WIDTH
    group_rollouts = q_heads // kv_heads
    head_queries = (
        query_vectors[0]
        .reshape(seq_rows, kv_heads, group_rollouts, HEAD_WIDTH)
        .transpose(1, 2, 0, 3)
    )
    gradient_heads = output_gradients.reshape(
        seq_rows, kv_heads, group_rollouts, HEAD_WIDTH
    ).transpose(1, 2, 0, 3)
    head_keys = keys_local.reshape(-1, kv_heads, HEAD_WIDTH).transpose(1, 0, 2)
    head_values = values_local.reshape(-1, kv_heads, HEAD_WIDTH).transpose(1, 0, 2)

    def scores_of(query_one, key_one):
        scores = (
            jnp.einsum("hsd,kd->hsk", query_one, key_one, preferred_element_type=jnp.float32)
            * scale_factor
        )
        return jnp.where(visible[None], scores, -1e30)

    def local_max(items):
        return jnp.max(scores_of(items[0], items[1]), -1)

    row_max = lax.pmax(lax.map(local_max, (head_queries, head_keys)), "trunk")

    def local_total(items):
        return jnp.sum(jnp.exp(scores_of(items[0], items[1]) - items[2][..., None]), -1)

    row_total = lax.psum(lax.map(local_total, (head_queries, head_keys, row_max)), "trunk")

    def probs_of(query_one, key_one, largest, total):
        return jnp.exp(scores_of(query_one, key_one) - largest[..., None]) / total[..., None]

    def local_delta(items):
        query_one, grad_one, key_one, value_one, largest, total = items
        probs = probs_of(query_one, key_one, largest, total)
        dprobs = jnp.einsum("hsd,kd->hsk", grad_one, value_one, preferred_element_type=jnp.float32)
        return jnp.sum(probs * dprobs, -1)

    stacked = (head_queries, gradient_heads, head_keys, head_values, row_max, row_total)
    delta = lax.psum(lax.map(local_delta, stacked), "trunk")

    def grads_of(items):
        query_one, grad_one, key_one, value_one, largest, total, delta_one = items
        probs = probs_of(query_one, key_one, largest, total)
        dprobs = jnp.einsum("hsd,kd->hsk", grad_one, value_one, preferred_element_type=jnp.float32)
        probs_low = probs.astype(jnp.bfloat16)
        dscores = (probs * (dprobs - delta_one[..., None]) * scale_factor).astype(jnp.bfloat16)
        key_gradient = jnp.einsum(
            "hsk,hsd->kd", dscores, query_one, preferred_element_type=jnp.float32
        )
        value_gradient = jnp.einsum(
            "hsk,hsd->kd", probs_low, grad_one, preferred_element_type=jnp.float32
        )
        return (dscores, key_gradient, value_gradient)

    def local_grads(items):
        dscores, key_gradient, value_gradient = grads_of(items)
        dquery = jnp.einsum("hsk,kd->hsd", dscores, items[2], preferred_element_type=jnp.float32)
        return (dquery, key_gradient, value_gradient)

    dquery, key_gradient, value_gradient = lax.map(local_grads, stacked + (delta,))
    dquery = dquery.transpose(2, 0, 1, 3).reshape(1, seq_rows, q_heads * HEAD_WIDTH)
    query_grad = lax.psum_scatter(
        dquery.astype(jnp.bfloat16), "trunk", scatter_dimension=1, tiled=True
    )
    key_gradient = key_gradient.transpose(1, 0, 2).reshape(-1, kv_heads * HEAD_WIDTH)
    value_gradient = value_gradient.transpose(1, 0, 2).reshape(-1, kv_heads * HEAD_WIDTH)
    trunk_key_grad, trunk_value_grad = (
        lax.psum_scatter(
            key_gradient[:slab_rows].astype(jnp.bfloat16), "branch", scatter_dimension=0, tiled=True
        ).astype(jnp.float32),
        lax.psum_scatter(
            value_gradient[:slab_rows].astype(jnp.bfloat16),
            "branch",
            scatter_dimension=0,
            tiled=True,
        ).astype(jnp.float32),
    )
    branch_key_grad = key_gradient[slab_rows:][None].astype(jnp.bfloat16)
    branch_value_grad = value_gradient[slab_rows:][None].astype(jnp.bfloat16)
    return (
        query_grad,
        trunk_key_grad.astype(jnp.bfloat16),
        trunk_value_grad.astype(jnp.bfloat16),
        branch_key_grad,
        branch_value_grad,
    )


MESH = pl.DeviceIdType.MESH
W = HEAD_WIDTH
NT = (((1,), (1,)), ((), ()))
TN = (((0,), (0,)), ((), ()))
HIDDEN = -1e30


def dot(lhs, rhs, dims=None):
    if dims is None:
        return jnp.dot(lhs, rhs, preferred_element_type=jnp.float32)
    return lax.dot_general(lhs, rhs, dims, preferred_element_type=jnp.float32)


def fused_kernel(
    forks,
    lengths,
    query,
    cotangent,
    branch_keys,
    branch_values,
    trunk_keys,
    trunk_values,
    query_grad,
    z_in,
    own_in,
    q_in,
    c_in,
    kv,
    own,
    q_rows,
    c_rows,
    scores,
    dprobs,
    dq_total,
    mine,
    x_out,
    x_in,
    z_out,
    own_out,
    dq_out,
    local_sem,
    z_send,
    z_recv,
    x_send,
    x_recv,
    back_send,
    back_recv,
):
    z = lax.axis_index("trunk")
    x = lax.axis_index("branch")
    head = lax.rem(z, 2)
    at = (z, z + 1 - 2 * head, lax.rem(z + 2, 4), 3 - z)
    other_x = {"branch": 1 - x}
    rows = query.shape[1]
    slab = trunk_keys.shape[0]
    group = query.shape[2] // 2 // W
    wide = group * W
    cols = 2 * group * rows
    scale = W ** (-0.5)

    def head_cols(index, width):
        return pl.ds(pl.multiple_of(index * width, width), width)

    barrier = pltpu.get_barrier_semaphore()
    for d in (1, 2, 3):
        pl.semaphore_signal(barrier, inc=1, device_id={"trunk": at[d]}, device_id_type=MESH)
    pl.semaphore_signal(barrier, inc=1, device_id=other_x, device_id_type=MESH)
    pl.semaphore_wait(barrier, 4)

    def remote(src, dst, send, recv, device):
        return pltpu.make_async_remote_copy(
            src_ref=src,
            dst_ref=dst,
            send_sem=send,
            recv_sem=recv,
            device_id=device,
            device_id_type=MESH,
        )

    mine_cols = head_cols(head, W)
    x_copies = {}
    first = []
    for n, ref in enumerate((trunk_keys, trunk_values)):
        first.append(
            remote(
                ref.at[:, mine_cols], kv.at[1, 0, n], x_send.at[0, n], x_recv.at[0, n], other_x
            )
        )
    x_copies[0] = first
    z_copies = {}
    for d in (1, 2, 3):
        sent = head_cols(lax.rem(at[d], 2), W)
        to = {"trunk": at[d]}
        z_copies[d] = [
            remote(ref.at[:, sent], kv.at[0, d, n], z_send.at[d, n], z_recv.at[d, n], to)
            for n, ref in enumerate((trunk_keys, trunk_values))
        ] + [
            remote(ref.at[0, :, sent], own.at[n, d], z_send.at[d, 2 + n], z_recv.at[d, 2 + n], to)
            for n, ref in enumerate((branch_keys, branch_values))
        ]
    pair_cols = head_cols(1 - head, wide)
    q_copies = [
        remote(
            ref.at[0, :, pair_cols], dst.at[1], z_send.at[0, n], z_recv.at[0, n], {"trunk": at[1]}
        )
        for n, (ref, dst) in enumerate(((query, q_in), (cotangent, c_in)))
    ]
    for copy in z_copies[1][:2] + x_copies[0] + z_copies[2][:2] + z_copies[3][:2]:
        copy.start()
    for copy in q_copies:
        copy.start()
    for d in (1, 2, 3):
        for copy in z_copies[d][2:]:
            copy.start()
    local = []
    for n, ref in enumerate((trunk_keys, trunk_values)):
        local.append(pltpu.make_async_copy(ref.at[:, mine_cols], kv.at[0, 0, n], local_sem.at[n]))
    for n, ref in enumerate((branch_keys, branch_values)):
        local.append(
            pltpu.make_async_copy(ref.at[0, :, mine_cols], own.at[n, 0], local_sem.at[2 + n])
        )
    for n, (ref, dst) in enumerate(((query, q_in), (cotangent, c_in))):
        local.append(
            pltpu.make_async_copy(
                ref.at[0, :, head_cols(head, wide)], dst.at[0], local_sem.at[4 + n]
            )
        )
    for copy in local:
        copy.start()

    for d in (1, 2, 3):
        for copy in z_copies[d][:2]:
            copy.wait_recv()
        x_copies[d] = [
            remote(kv.at[0, d], kv.at[1, d], x_send.at[d, 0], x_recv.at[d, 0], other_x)
        ]
        x_copies[d][0].start()
    for copy in local:
        copy.wait()
    for copy in q_copies:
        copy.wait_recv()

    fork = forks[0]
    length = lengths[0]
    row_iota = lax.broadcasted_iota(jnp.int32, (rows, W), 0)
    for e in (0, 1):
        live = (row_iota + at[e] * rows < length).astype(jnp.float32)
        for g in range(group):
            start = (e * group + g) * rows
            q_rows[start : start + rows, :] = q_in[e, :, g * W : (g + 1) * W]
            part = c_in[e, :, g * W : (g + 1) * W].astype(jnp.float32) * live
            c_rows[start : start + rows, :] = part.astype(jnp.bfloat16)

    col = lax.broadcasted_iota(jnp.int32, (1, cols), 1)
    half = group * rows
    col_pos = jnp.where(col < half, at[0], at[1]) * rows + lax.rem(col, rows)
    slab_iota = lax.broadcasted_iota(jnp.int32, (slab, 1), 0)

    blocks = [(r, d) for r in (0, 1) for d in range(4)]
    base_of = {block: i * slab for i, block in enumerate(blocks)}
    own_base = len(blocks) * slab
    own_rows = 4 * rows

    def score(base, size, key, value, seen):
        part = dot(key, q_rows[...], NT) * scale
        part = jnp.where(seen, part, HIDDEN)
        scores[base : base + size, :] = part
        dprobs[base : base + size, :] = dot(value, c_rows[...], NT)
        return jnp.max(part, 0, keepdims=True)

    def trunk_score(r, d):
        side = x if r == 0 else 1 - x
        seen = slab_iota + (at[d] * 2 + side) * slab < fork
        return score(base_of[r, d], slab, kv[r, d, 0], kv[r, d, 1], seen)

    largest = trunk_score(0, 0)
    for d in (1, 2, 3):
        largest = jnp.maximum(largest, trunk_score(0, d))
    for d in (1, 2, 3):
        for copy in z_copies[d][2:]:
            copy.wait_recv()
    own_iota = lax.broadcasted_iota(jnp.int32, (rows, 1), 0)
    own_pos = jnp.concatenate([own_iota + at[d] * rows for d in range(4)], 0)
    own_key = own[0].reshape(own_rows, W)
    own_value = own[1].reshape(own_rows, W)
    largest = jnp.maximum(
        largest,
        score(
            own_base, own_rows, own_key, own_value, (own_pos <= col_pos) & (own_pos < length)
        ),
    )
    for d in range(4):
        for copy in x_copies[d]:
            copy.wait_recv()
        largest = jnp.maximum(largest, trunk_score(1, d))

    total = jnp.zeros((1, cols), jnp.float32)
    delta = jnp.zeros((1, cols), jnp.float32)
    for base in range(0, own_base + own_rows, W):
        weights = jnp.exp(scores[base : base + W, :] - largest)
        scores[base : base + W, :] = weights
        total += jnp.sum(weights, 0, keepdims=True)
        delta += jnp.sum(weights * dprobs[base : base + W, :], 0, keepdims=True)
    inverse = 1.0 / total
    delta = delta * inverse
    dq_total[...] = jnp.zeros_like(dq_total)

    def grads(base, size, key):
        probs = scores[base : base + size, :] * inverse
        low = probs.astype(jnp.bfloat16)
        dscores = (probs * (dprobs[base : base + size, :] - delta) * scale).astype(jnp.bfloat16)
        dq_total[...] += dot(key, dscores, TN)
        return dot(dscores, q_rows[...]), dot(low, c_rows[...])

    back = {}
    for d in (3, 2, 1, 0):
        pair = grads(base_of[1, d], slab, kv[1, d, 0])
        for n in (0, 1):
            x_out[d, n] = pair[n].astype(jnp.bfloat16)
        back[d] = remote(x_out.at[d], x_in.at[d], back_send.at[d], back_recv.at[d], other_x)
        back[d].start()
    pair = grads(own_base, own_rows, own_key)
    for n in (0, 1):
        mine_part = pair[n].astype(jnp.bfloat16)
        for d in range(4):
            own_out[d, n] = mine_part[d * rows : (d + 1) * rows, :]
    for d in (3, 2, 1):
        back[4 + d] = remote(
            own_out.at[d],
            own_in.at[d],
            back_send.at[4 + d],
            back_recv.at[4 + d],
            {"trunk": at[d]},
        )
        back[4 + d].start()
    kept = [pltpu.make_async_copy(own_out.at[0], own_in.at[0], local_sem.at[0])]
    kept[0].start()
    for d in (3, 2, 1, 0):
        pair = grads(base_of[0, d], slab, kv[0, d, 0])
        for n in (0, 1):
            mine[d, n] = pair[n]
    dq = dq_total[...].T.astype(jnp.bfloat16)
    for e in (1, 0):
        for g in range(group):
            start = e * half + g * rows
            dq_out[e, :, g * W : (g + 1) * W] = dq[start : start + rows, :]
    dq_cols = query_grad.at[0, :, head_cols(head, wide)]
    back[4] = remote(dq_out.at[1], dq_cols, back_send.at[4], back_recv.at[4], {"trunk": at[1]})
    back[4].start()
    kept.append(pltpu.make_async_copy(dq_out.at[0], dq_cols, local_sem.at[1]))
    kept[1].start()
    for d in (3, 2, 1, 0):
        back[d].wait_recv()
        z_out[d] = (mine[d] + x_in[d].astype(jnp.float32)).astype(jnp.bfloat16)
        if d == 0:
            kept.append(pltpu.make_async_copy(z_out.at[0], z_in.at[0], local_sem.at[2]))
            kept[2].start()
        else:
            back[8 + d] = remote(
                z_out.at[d], z_in.at[d], back_send.at[8 + d], back_recv.at[8 + d], {"trunk": at[d]}
            )
            back[8 + d].start()
    for d in (3, 2, 1):
        back[4 + d].wait_recv()
        back[8 + d].wait_recv()
    back[4].wait_recv()
    for copy in q_copies + sum(z_copies.values(), []) + sum(x_copies.values(), []):
        copy.wait_send()
    for copy in back.values():
        copy.wait_send()
    for copy in kept:
        copy.wait()


def owners_sum(
    query_in,
    z_in,
    own_in,
    query_grad,
    trunk_key_grad,
    trunk_value_grad,
    branch_key_grad,
    branch_value_grad,
):
    head = lax.rem(lax.axis_index("trunk"), 2)
    f32 = jnp.float32
    query_grad[...] = query_in[...]
    for a, b, which in ((0, 2, head), (1, 3, 1 - head)):
        at = pl.ds(pl.multiple_of(which * W, W), W)
        for n, ref in enumerate((trunk_key_grad, trunk_value_grad)):
            ref[:, at] = (z_in[a, n].astype(f32) + z_in[b, n].astype(f32)).astype(jnp.bfloat16)
        for n, ref in enumerate((branch_key_grad, branch_value_grad)):
            ref[0, :, at] = (own_in[a, n].astype(f32) + own_in[b, n].astype(f32)).astype(
                jnp.bfloat16
            )


def fused(
    query,
    cotangent,
    branch_keys,
    rollout_value_rows,
    trunk_keys,
    shared_trunk_values,
    forks,
    lengths,
):
    rows = query.shape[1]
    slab = trunk_keys.shape[0]
    wide = query.shape[2] // 2
    cols = 2 * rows * (wide // W)
    keys = 8 * slab + 4 * rows
    bf16, f32 = jnp.bfloat16, jnp.float32
    smem = pl.BlockSpec(memory_space=pltpu.SMEM)
    anywhere = pl.BlockSpec(memory_space=pl.ANY)
    vmem = pl.BlockSpec(memory_space=pltpu.VMEM)

    def like(a):
        return jax.ShapeDtypeStruct(a.shape, a.dtype)

    dma = pltpu.SemaphoreType.DMA
    shares = pl.pallas_call(
        fused_kernel,
        out_shape=(
            like(query),
            jax.ShapeDtypeStruct((4, 2, slab, W), bf16),
            jax.ShapeDtypeStruct((4, 2, rows, W), bf16),
        ),
        in_specs=[smem] * 2 + [anywhere] * 6,
        out_specs=(anywhere,) * 3,
        scratch_shapes=[
            pltpu.VMEM((2, rows, wide), bf16),
            pltpu.VMEM((2, rows, wide), bf16),
            pltpu.VMEM((2, 4, 2, slab, W), bf16),
            pltpu.VMEM((2, 4, rows, W), bf16),
            pltpu.VMEM((cols, W), bf16),
            pltpu.VMEM((cols, W), bf16),
            pltpu.VMEM((keys, cols), f32),
            pltpu.VMEM((keys, cols), f32),
            pltpu.VMEM((W, cols), f32),
            pltpu.VMEM((4, 2, slab, W), f32),
            pltpu.VMEM((4, 2, slab, W), bf16),
            pltpu.VMEM((4, 2, slab, W), bf16),
            pltpu.VMEM((4, 2, slab, W), bf16),
            pltpu.VMEM((4, 2, rows, W), bf16),
            pltpu.VMEM((2, rows, wide), bf16),
            dma((6,)),
            dma((4, 4)),
            dma((4, 4)),
            dma((4, 2)),
            dma((4, 2)),
            dma((12,)),
            dma((12,)),
        ],
        compiler_params=pltpu.CompilerParams(
            collective_id=0, has_side_effects=True, vmem_limit_bytes=60 * 1024 * 1024
        ),
        cost_estimate=pl.CostEstimate(
            flops=10 * keys * cols * W, bytes_accessed=2**20, transcendentals=keys * cols
        ),
    )(
        forks,
        lengths,
        query,
        cotangent,
        branch_keys,
        rollout_value_rows,
        trunk_keys,
        shared_trunk_values,
    )
    return pl.pallas_call(
        owners_sum,
        out_shape=tuple(
            like(a) for a in (query, trunk_keys, shared_trunk_values, branch_keys, rollout_value_rows)
        ),
        in_specs=[vmem] * 3,
        out_specs=(vmem,) * 5,
        compiler_params=pltpu.CompilerParams(vmem_limit_bytes=60 * 1024 * 1024),
    )(*shares)


def plan_of(mesh):
    if mesh.shape["trunk"] == 4 and mesh.shape["branch"] == 2:
        return fused
    return shards


def solution(mesh):
    return jax.shard_map(
        plan_of(mesh),
        mesh=mesh,
        in_specs=(
            P(("groups", "branch"), "trunk", "tensor"),
            P(("groups", "branch"), "trunk", "tensor"),
            P(("groups", "branch"), "trunk", "tensor"),
            P(("groups", "branch"), "trunk", "tensor"),
            P(("groups", "trunk", "branch"), "tensor"),
            P(("groups", "trunk", "branch"), "tensor"),
            P(("groups", "branch")),
            P(("groups", "branch")),
        ),
        out_specs=(
            P(("groups", "branch"), "trunk", "tensor"),
            P(("groups", "trunk", "branch"), "tensor"),
            P(("groups", "trunk", "branch"), "tensor"),
            P(("groups", "branch"), "trunk", "tensor"),
            P(("groups", "branch"), "trunk", "tensor"),
        ),
        check_vma=False,
    )
```

```python
import functools

import jax
import jax.numpy as jnp
from jax import lax
from jax.experimental import pallas as pl
from jax.experimental.pallas import tpu as pltpu
from jax.sharding import PartitionSpec as P

HEAD_WIDTH = 128


def shards(
    query,
    cotangent,
    branch_keys,
    rollout_value_rows,
    trunk_keys,
    shared_trunk_values,
    forks,
    lengths,
):
    scale_factor = HEAD_WIDTH ** (-0.5)
    query_vectors, output_gradients = (
        lax.all_gather(query, "trunk", axis=1, tiled=True),
        lax.all_gather(cotangent, "trunk", axis=1, tiled=True),
    )
    slab_keys, slab_values = (
        lax.all_gather(trunk_keys, "branch", axis=0, tiled=True),
        lax.all_gather(shared_trunk_values, "branch", axis=0, tiled=True),
    )
    trunk_index = lax.axis_index("trunk")
    slab_rows = slab_keys.shape[0]
    block_rows = branch_keys.shape[1]
    seq_rows = query_vectors.shape[1]
    fork_point = forks[0]
    length = lengths[0]
    positions = jnp.arange(seq_rows, dtype=jnp.int32)
    is_valid = positions < length
    output_gradients = output_gradients[0] * is_valid[:, None].astype(jnp.bfloat16)
    keys_local = jnp.concatenate([slab_keys, branch_keys[0]], 0)
    values_local = jnp.concatenate([slab_values, rollout_value_rows[0]], 0)
    slab_positions = trunk_index * slab_rows + jnp.arange(slab_rows, dtype=jnp.int32)
    block_positions = trunk_index * block_rows + jnp.arange(block_rows, dtype=jnp.int32)
    trunk_seen = jnp.broadcast_to(slab_positions[None, :] < fork_point, (seq_rows, slab_rows))
    own_seen = (block_positions[None, :] <= positions[:, None]) & (
        block_positions[None, :] < length
    )
    visible = jnp.concatenate([trunk_seen, own_seen], 1)
    kv_heads = keys_local.shape[1] // HEAD_WIDTH
    q_heads = query_vectors.shape[2] // HEAD_WIDTH
    group_rollouts = q_heads // kv_heads
    head_queries = (
        query_vectors[0]
        .reshape(seq_rows, kv_heads, group_rollouts, HEAD_WIDTH)
        .transpose(1, 2, 0, 3)
    )
    gradient_heads = output_gradients.reshape(
        seq_rows, kv_heads, group_rollouts, HEAD_WIDTH
    ).transpose(1, 2, 0, 3)
    head_keys = keys_local.reshape(-1, kv_heads, HEAD_WIDTH).transpose(1, 0, 2)
    head_values = values_local.reshape(-1, kv_heads, HEAD_WIDTH).transpose(1, 0, 2)

    def scores_of(query_one, key_one):
        scores = (
            jnp.einsum("hsd,kd->hsk", query_one, key_one, preferred_element_type=jnp.float32)
            * scale_factor
        )
        return jnp.where(visible[None], scores, -1e30)

    def local_max(items):
        return jnp.max(scores_of(items[0], items[1]), -1)

    row_max = lax.pmax(lax.map(local_max, (head_queries, head_keys)), "trunk")

    def local_total(items):
        return jnp.sum(jnp.exp(scores_of(items[0], items[1]) - items[2][..., None]), -1)

    row_total = lax.psum(lax.map(local_total, (head_queries, head_keys, row_max)), "trunk")

    def probs_of(query_one, key_one, largest, total):
        return jnp.exp(scores_of(query_one, key_one) - largest[..., None]) / total[..., None]

    def local_delta(items):
        query_one, grad_one, key_one, value_one, largest, total = items
        probs = probs_of(query_one, key_one, largest, total)
        dprobs = jnp.einsum("hsd,kd->hsk", grad_one, value_one, preferred_element_type=jnp.float32)
        return jnp.sum(probs * dprobs, -1)

    stacked = (head_queries, gradient_heads, head_keys, head_values, row_max, row_total)
    delta = lax.psum(lax.map(local_delta, stacked), "trunk")

    def grads_of(items):
        query_one, grad_one, key_one, value_one, largest, total, delta_one = items
        probs = probs_of(query_one, key_one, largest, total)
        dprobs = jnp.einsum("hsd,kd->hsk", grad_one, value_one, preferred_element_type=jnp.float32)
        probs_low = probs.astype(jnp.bfloat16)
        dscores = (probs * (dprobs - delta_one[..., None]) * scale_factor).astype(jnp.bfloat16)
        key_gradient = jnp.einsum(
            "hsk,hsd->kd", dscores, query_one, preferred_element_type=jnp.float32
        )
        value_gradient = jnp.einsum(
            "hsk,hsd->kd", probs_low, grad_one, preferred_element_type=jnp.float32
        )
        return (dscores, key_gradient, value_gradient)

    def local_grads(items):
        dscores, key_gradient, value_gradient = grads_of(items)
        dquery = jnp.einsum("hsk,kd->hsd", dscores, items[2], preferred_element_type=jnp.float32)
        return (dquery, key_gradient, value_gradient)

    dquery, key_gradient, value_gradient = lax.map(local_grads, stacked + (delta,))
    dquery = dquery.transpose(2, 0, 1, 3).reshape(1, seq_rows, q_heads * HEAD_WIDTH)
    query_grad = lax.psum_scatter(
        dquery.astype(jnp.bfloat16), "trunk", scatter_dimension=1, tiled=True
    )
    key_gradient = key_gradient.transpose(1, 0, 2).reshape(-1, kv_heads * HEAD_WIDTH)
    value_gradient = value_gradient.transpose(1, 0, 2).reshape(-1, kv_heads * HEAD_WIDTH)
    trunk_key_grad, trunk_value_grad = (
        lax.psum_scatter(
            key_gradient[:slab_rows].astype(jnp.bfloat16), "branch", scatter_dimension=0, tiled=True
        ).astype(jnp.float32),
        lax.psum_scatter(
            value_gradient[:slab_rows].astype(jnp.bfloat16),
            "branch",
            scatter_dimension=0,
            tiled=True,
        ).astype(jnp.float32),
    )
    branch_key_grad = key_gradient[slab_rows:][None].astype(jnp.bfloat16)
    branch_value_grad = value_gradient[slab_rows:][None].astype(jnp.bfloat16)
    return (
        query_grad,
        trunk_key_grad.astype(jnp.bfloat16),
        trunk_value_grad.astype(jnp.bfloat16),
        branch_key_grad,
        branch_value_grad,
    )


MESH = pl.DeviceIdType.MESH
W = HEAD_WIDTH
NT = (((1,), (1,)), ((), ()))
TN = (((0,), (0,)), ((), ()))
HIDDEN = -1e30


def dot(lhs, rhs, dims=None):
    if dims is None:
        return jnp.dot(lhs, rhs, preferred_element_type=jnp.float32)
    return lax.dot_general(lhs, rhs, dims, preferred_element_type=jnp.float32)


def fused_kernel(
    forks,
    lengths,
    query,
    cotangent,
    branch_keys,
    branch_values,
    trunk_keys,
    trunk_values,
    query_grad,
    z_in,
    own_in,
    kv_here,
    q_here,
    own_here,
    q_in,
    kv,
    own,
    q_rows,
    c_rows,
    scores,
    dprobs,
    dq_total,
    mine,
    x_out,
    x_in,
    z_out,
    own_out,
    dq_out,
    limits_out,
    limits_in,
    local_sem,
    z_send,
    z_recv,
    x_send,
    x_recv,
    back_send,
    back_recv,
):
    z = lax.axis_index("trunk")
    x = lax.axis_index("branch")
    core = lax.axis_index("tensor")
    head = lax.rem(z, 2)
    at = (z, z + 1 - 2 * head, lax.rem(z + 2, 4), 3 - z)
    workers = [{"trunk": there, "branch": core, "tensor": 1 - x} for there in at]
    homes = [{"trunk": there, "branch": 1 - core, "tensor": x} for there in at]
    twin = {"tensor": 1 - core}
    rows = query.shape[1]
    slab = trunk_keys.shape[0]
    group = query.shape[2] // 2 // W
    wide = group * W
    cols = 2 * group * rows
    scale = W ** (-0.5)

    def head_cols(index, width):
        return pl.ds(pl.multiple_of(index * width, width), width)

    local = []
    for i in (0, 1):
        for n, ref in enumerate((trunk_keys, trunk_values)):
            local.append((ref.at[:, pl.ds(i * W, W)], kv_here.at[i, n]))
        for n, ref in enumerate((query, cotangent)):
            local.append((ref.at[0, :, pl.ds(i * wide, wide)], q_here.at[i, n]))
        for n, ref in enumerate((branch_keys, branch_values)):
            local.append((ref.at[0, :, pl.ds(i * W, W)], own_here.at[i, n]))
    local = [
        pltpu.make_async_copy(src, dst, local_sem.at[k]) for k, (src, dst) in enumerate(local)
    ]
    for copy in local:
        copy.start()
    barrier = pltpu.get_barrier_semaphore()
    for device in workers + homes:
        pl.semaphore_signal(barrier, inc=1, device_id=device, device_id_type=MESH)
    pl.semaphore_wait(barrier, len(workers + homes))

    def remote(src, dst, send, recv, device):
        return pltpu.make_async_remote_copy(
            src_ref=src,
            dst_ref=dst,
            send_sem=send,
            recv_sem=recv,
            device_id=device,
            device_id_type=MESH,
        )

    limits_out[0] = jnp.full(limits_out.shape[1:], forks[0], jnp.int32)
    limits_out[1] = jnp.full(limits_out.shape[1:], lengths[0], jnp.int32)
    z_copies = {}
    for d in range(4):
        sent = lax.rem(at[d], 2)
        z_copies[d] = [
            remote(here.at[sent], there(d), z_send.at[d, n], z_recv.at[d, n], workers[d])
            for n, (here, there) in enumerate(
                (
                    (kv_here, lambda d: kv.at[0, :, d]),
                    (own_here, lambda d: own.at[:, d]),
                    (q_here, lambda d: q_in.at[d]),
                )
            )
            if n < 2 or d < 2
        ]
    limits = remote(limits_out, limits_in, z_send.at[2, 2], z_recv.at[2, 2], workers[0])
    for copy in local:
        copy.wait()
    limits.start()
    for d in (1, 2, 3, 0):
        z_copies[d][0].start()
    for d in (1, 2, 3, 0):
        z_copies[d][1].start()
    for d in (1, 0):
        z_copies[d][2].start()

    x_copies = {}
    for d in (1, 2, 3, 0):
        z_copies[d][0].wait_recv()
        x_copies[d] = remote(kv.at[0, :, d], kv.at[1, :, d], x_send.at[d], x_recv.at[d], twin)
        x_copies[d].start()
    limits.wait_recv()
    for e in (0, 1):
        z_copies[e][2].wait_recv()

    fork = limits_in[0, 0:1, 0:1]
    length = limits_in[1, 0:1, 0:1]
    row_iota = lax.broadcasted_iota(jnp.int32, (rows, W), 0)
    for e in (0, 1):
        live = (row_iota + at[e] * rows < length).astype(jnp.float32)
        for g in range(group):
            start = (e * group + g) * rows
            q_rows[start : start + rows, :] = q_in[e, 0, :, g * W : (g + 1) * W]
            part = q_in[e, 1, :, g * W : (g + 1) * W].astype(jnp.float32) * live
            c_rows[start : start + rows, :] = part.astype(jnp.bfloat16)

    col = lax.broadcasted_iota(jnp.int32, (1, cols), 1)
    half = group * rows
    col_pos = jnp.where(col < half, at[0], at[1]) * rows + lax.rem(col, rows)
    slab_iota = lax.broadcasted_iota(jnp.int32, (slab, 1), 0)

    own_base = 8 * slab
    own_rows = 4 * rows

    def score(base, size, key, value, seen):
        part = dot(key, q_rows[...], NT) * scale
        part = jnp.where(seen, part, HIDDEN)
        scores[base : base + size, :] = part
        dprobs[base : base + size, :] = dot(value, c_rows[...], NT)
        return jnp.max(part, 0, keepdims=True)

    def trunk_score(r):
        side = 1 - core if r == 0 else core
        pos = jnp.concatenate([slab_iota + (there * 2 + side) * slab for there in at], 0)
        key, value = [kv[r, n].reshape(4 * slab, W) for n in (0, 1)]
        return score(r * 4 * slab, 4 * slab, key, value, pos < fork)

    largest = trunk_score(0)
    for d in range(4):
        z_copies[d][1].wait_recv()
    own_iota = lax.broadcasted_iota(jnp.int32, (rows, 1), 0)
    own_pos = jnp.concatenate([own_iota + at[d] * rows for d in range(4)], 0)
    own_key = own[0].reshape(own_rows, W)
    own_value = own[1].reshape(own_rows, W)
    largest = jnp.maximum(
        largest,
        score(
            own_base, own_rows, own_key, own_value, (own_pos <= col_pos) & (own_pos < length)
        ),
    )
    for d in (1, 2, 3, 0):
        x_copies[d].wait_recv()
    largest = jnp.maximum(largest, trunk_score(1))

    total = jnp.zeros((1, cols), jnp.float32)
    delta = jnp.zeros((1, cols), jnp.float32)
    for base in range(0, own_base + own_rows, W):
        weights = jnp.exp(scores[base : base + W, :] - largest)
        scores[base : base + W, :] = weights
        total += jnp.sum(weights, 0, keepdims=True)
        delta += jnp.sum(weights * dprobs[base : base + W, :], 0, keepdims=True)
    inverse = 1.0 / total
    delta = delta * inverse
    dq_total[...] = jnp.zeros_like(dq_total)

    def grads(base, size, key):
        probs = scores[base : base + size, :] * inverse
        low = probs.astype(jnp.bfloat16)
        dscores = (probs * (dprobs[base : base + size, :] - delta) * scale).astype(jnp.bfloat16)
        dq_total[...] += dot(key, dscores, TN)
        return dot(dscores, q_rows[...]), dot(low, c_rows[...])

    back = {}
    for d in (3, 2, 1, 0):
        if d in (3, 1):
            key = kv[1, 0, d - 1 : d + 1].reshape(2 * slab, W)
            pair = grads((3 + d) * slab, 2 * slab, key)
        for n in (0, 1):
            part = pair[n][d % 2 * slab : (d % 2 + 1) * slab]
            x_out[d, n] = part.astype(jnp.bfloat16)
        back[d] = remote(x_out.at[d], x_in.at[d], back_send.at[d], back_recv.at[d], twin)
        back[d].start()
    pair = grads(own_base, own_rows, own_key)
    for n in (0, 1):
        mine_part = pair[n].astype(jnp.bfloat16)
        for d in range(4):
            own_out[d, n] = mine_part[d * rows : (d + 1) * rows, :]
    for d in (3, 2, 1, 0):
        back[4 + d] = remote(
            own_out.at[d], own_in.at[d], back_send.at[4 + d], back_recv.at[4 + d], homes[d]
        )
        back[4 + d].start()
    pair = grads(0, 4 * slab, kv[0, 0].reshape(4 * slab, W))
    for d in range(4):
        for n in (0, 1):
            mine[d, n] = pair[n][d * slab : (d + 1) * slab]
    dq = dq_total[...].T.astype(jnp.bfloat16)
    for e in (1, 0):
        for g in range(group):
            start = e * half + g * rows
            dq_out[e, :, g * W : (g + 1) * W] = dq[start : start + rows, :]
    for e in (1, 0):
        back[12 + e] = remote(
            dq_out.at[e],
            query_grad.at[0, :, head_cols(head, wide)],
            back_send.at[12 + e],
            back_recv.at[12 + e],
            homes[e],
        )
        back[12 + e].start()
    for d in (3, 2, 1, 0):
        back[d].wait_recv()
        z_out[d] = (mine[d] + x_in[d].astype(jnp.float32)).astype(jnp.bfloat16)
        back[8 + d] = remote(
            z_out.at[d], z_in.at[d], back_send.at[8 + d], back_recv.at[8 + d], homes[d]
        )
        back[8 + d].start()
    for key, copy in back.items():
        if key >= 4:
            copy.wait_recv()
    limits.wait_send()
    for copy in sum(z_copies.values(), []):
        copy.wait_send()
    for copies in (x_copies, back):
        for copy in copies.values():
            copy.wait_send()


def owners_sum(
    query_in,
    z_in,
    own_in,
    query_grad,
    trunk_key_grad,
    trunk_value_grad,
    branch_key_grad,
    branch_value_grad,
):
    head = lax.rem(lax.axis_index("trunk"), 2)
    f32 = jnp.float32
    query_grad[...] = query_in[...]
    for a, b, which in ((0, 2, head), (1, 3, 1 - head)):
        at = pl.ds(pl.multiple_of(which * W, W), W)
        for n, ref in enumerate((trunk_key_grad, trunk_value_grad)):
            ref[:, at] = (z_in[a, n].astype(f32) + z_in[b, n].astype(f32)).astype(jnp.bfloat16)
        for n, ref in enumerate((branch_key_grad, branch_value_grad)):
            ref[0, :, at] = (own_in[a, n].astype(f32) + own_in[b, n].astype(f32)).astype(
                jnp.bfloat16
            )


def fused(
    query,
    cotangent,
    branch_keys,
    rollout_value_rows,
    trunk_keys,
    shared_trunk_values,
    forks,
    lengths,
):
    rows = query.shape[1]
    slab = trunk_keys.shape[0]
    wide = query.shape[2] // 2
    cols = 2 * rows * (wide // W)
    keys = 8 * slab + 4 * rows
    bf16, f32 = jnp.bfloat16, jnp.float32
    smem = pl.BlockSpec(memory_space=pltpu.SMEM)
    anywhere = pl.BlockSpec(memory_space=pl.ANY)
    vmem = pl.BlockSpec(memory_space=pltpu.VMEM)

    def like(a):
        return jax.ShapeDtypeStruct(a.shape, a.dtype)

    dma = pltpu.SemaphoreType.DMA
    shares = pl.pallas_call(
        fused_kernel,
        out_shape=(
            like(query),
            jax.ShapeDtypeStruct((4, 2, slab, W), bf16),
            jax.ShapeDtypeStruct((4, 2, rows, W), bf16),
        ),
        in_specs=[smem] * 2 + [anywhere] * 6,
        out_specs=(anywhere,) * 3,
        scratch_shapes=[
            pltpu.VMEM((2, 2, slab, W), bf16),
            pltpu.VMEM((2, 2, rows, wide), bf16),
            pltpu.VMEM((2, 2, rows, W), bf16),
            pltpu.VMEM((2, 2, rows, wide), bf16),
            pltpu.VMEM((2, 2, 4, slab, W), bf16),
            pltpu.VMEM((2, 4, rows, W), bf16),
            pltpu.VMEM((cols, W), bf16),
            pltpu.VMEM((cols, W), bf16),
            pltpu.VMEM((keys, cols), f32),
            pltpu.VMEM((keys, cols), f32),
            pltpu.VMEM((W, cols), f32),
            pltpu.VMEM((4, 2, slab, W), f32),
            pltpu.VMEM((4, 2, slab, W), bf16),
            pltpu.VMEM((4, 2, slab, W), bf16),
            pltpu.VMEM((4, 2, slab, W), bf16),
            pltpu.VMEM((4, 2, rows, W), bf16),
            pltpu.VMEM((2, rows, wide), bf16),
            pltpu.VMEM((2, 8, W), jnp.int32),
            pltpu.VMEM((2, 8, W), jnp.int32),
            dma((12,)),
            dma((4, 3)),
            dma((4, 3)),
            dma((4,)),
            dma((4,)),
            dma((14,)),
            dma((14,)),
        ],
        compiler_params=pltpu.CompilerParams(
            collective_id=0, has_side_effects=True, vmem_limit_bytes=60 * 1024 * 1024
        ),
        cost_estimate=pl.CostEstimate(
            flops=10 * keys * cols * W, bytes_accessed=2**20, transcendentals=keys * cols
        ),
    )(
        forks,
        lengths,
        query,
        cotangent,
        branch_keys,
        rollout_value_rows,
        trunk_keys,
        shared_trunk_values,
    )
    return pl.pallas_call(
        owners_sum,
        out_shape=tuple(
            like(a) for a in (query, trunk_keys, shared_trunk_values, branch_keys, rollout_value_rows)
        ),
        in_specs=[vmem] * 3,
        out_specs=(vmem,) * 5,
        compiler_params=pltpu.CompilerParams(vmem_limit_bytes=60 * 1024 * 1024),
    )(*shares)


def plan_of(mesh):
    if mesh.shape["trunk"] == 4 and mesh.shape["branch"] == 2 and mesh.shape["tensor"] == 2:
        return fused
    return shards


def solution(mesh):
    return jax.shard_map(
        plan_of(mesh),
        mesh=mesh,
        in_specs=(
            P(("groups", "branch"), "trunk", "tensor"),
            P(("groups", "branch"), "trunk", "tensor"),
            P(("groups", "branch"), "trunk", "tensor"),
            P(("groups", "branch"), "trunk", "tensor"),
            P(("groups", "trunk", "branch"), "tensor"),
            P(("groups", "trunk", "branch"), "tensor"),
            P(("groups", "branch")),
            P(("groups", "branch")),
        ),
        out_specs=(
            P(("groups", "branch"), "trunk", "tensor"),
            P(("groups", "trunk", "branch"), "tensor"),
            P(("groups", "trunk", "branch"), "tensor"),
            P(("groups", "branch"), "trunk", "tensor"),
            P(("groups", "branch"), "trunk", "tensor"),
        ),
        check_vma=False,
    )
```

```python
import functools

import jax
import jax.numpy as jnp
from jax import lax
from jax.experimental import pallas as pl
from jax.experimental.pallas import tpu as pltpu
from jax.sharding import PartitionSpec as P

HEAD_WIDTH = 128


def shards(
    query,
    cotangent,
    branch_keys,
    rollout_value_rows,
    trunk_keys,
    shared_trunk_values,
    forks,
    lengths,
):
    scale_factor = HEAD_WIDTH ** (-0.5)
    query_vectors, output_gradients = (
        lax.all_gather(query, "trunk", axis=1, tiled=True),
        lax.all_gather(cotangent, "trunk", axis=1, tiled=True),
    )
    slab_keys, slab_values = (
        lax.all_gather(trunk_keys, "branch", axis=0, tiled=True),
        lax.all_gather(shared_trunk_values, "branch", axis=0, tiled=True),
    )
    trunk_index = lax.axis_index("trunk")
    slab_rows = slab_keys.shape[0]
    block_rows = branch_keys.shape[1]
    seq_rows = query_vectors.shape[1]
    fork_point = forks[0]
    length = lengths[0]
    positions = jnp.arange(seq_rows, dtype=jnp.int32)
    is_valid = positions < length
    output_gradients = output_gradients[0] * is_valid[:, None].astype(jnp.bfloat16)
    keys_local = jnp.concatenate([slab_keys, branch_keys[0]], 0)
    values_local = jnp.concatenate([slab_values, rollout_value_rows[0]], 0)
    slab_positions = trunk_index * slab_rows + jnp.arange(slab_rows, dtype=jnp.int32)
    block_positions = trunk_index * block_rows + jnp.arange(block_rows, dtype=jnp.int32)
    trunk_seen = jnp.broadcast_to(slab_positions[None, :] < fork_point, (seq_rows, slab_rows))
    own_seen = (block_positions[None, :] <= positions[:, None]) & (
        block_positions[None, :] < length
    )
    visible = jnp.concatenate([trunk_seen, own_seen], 1)
    kv_heads = keys_local.shape[1] // HEAD_WIDTH
    q_heads = query_vectors.shape[2] // HEAD_WIDTH
    group_rollouts = q_heads // kv_heads
    head_queries = (
        query_vectors[0]
        .reshape(seq_rows, kv_heads, group_rollouts, HEAD_WIDTH)
        .transpose(1, 2, 0, 3)
    )
    gradient_heads = output_gradients.reshape(
        seq_rows, kv_heads, group_rollouts, HEAD_WIDTH
    ).transpose(1, 2, 0, 3)
    head_keys = keys_local.reshape(-1, kv_heads, HEAD_WIDTH).transpose(1, 0, 2)
    head_values = values_local.reshape(-1, kv_heads, HEAD_WIDTH).transpose(1, 0, 2)

    def scores_of(query_one, key_one):
        scores = (
            jnp.einsum("hsd,kd->hsk", query_one, key_one, preferred_element_type=jnp.float32)
            * scale_factor
        )
        return jnp.where(visible[None], scores, -1e30)

    def local_max(items):
        return jnp.max(scores_of(items[0], items[1]), -1)

    row_max = lax.pmax(lax.map(local_max, (head_queries, head_keys)), "trunk")

    def local_total(items):
        return jnp.sum(jnp.exp(scores_of(items[0], items[1]) - items[2][..., None]), -1)

    row_total = lax.psum(lax.map(local_total, (head_queries, head_keys, row_max)), "trunk")

    def probs_of(query_one, key_one, largest, total):
        return jnp.exp(scores_of(query_one, key_one) - largest[..., None]) / total[..., None]

    def local_delta(items):
        query_one, grad_one, key_one, value_one, largest, total = items
        probs = probs_of(query_one, key_one, largest, total)
        dprobs = jnp.einsum("hsd,kd->hsk", grad_one, value_one, preferred_element_type=jnp.float32)
        return jnp.sum(probs * dprobs, -1)

    stacked = (head_queries, gradient_heads, head_keys, head_values, row_max, row_total)
    delta = lax.psum(lax.map(local_delta, stacked), "trunk")

    def grads_of(items):
        query_one, grad_one, key_one, value_one, largest, total, delta_one = items
        probs = probs_of(query_one, key_one, largest, total)
        dprobs = jnp.einsum("hsd,kd->hsk", grad_one, value_one, preferred_element_type=jnp.float32)
        probs_low = probs.astype(jnp.bfloat16)
        dscores = (probs * (dprobs - delta_one[..., None]) * scale_factor).astype(jnp.bfloat16)
        key_gradient = jnp.einsum(
            "hsk,hsd->kd", dscores, query_one, preferred_element_type=jnp.float32
        )
        value_gradient = jnp.einsum(
            "hsk,hsd->kd", probs_low, grad_one, preferred_element_type=jnp.float32
        )
        return (dscores, key_gradient, value_gradient)

    def local_grads(items):
        dscores, key_gradient, value_gradient = grads_of(items)
        dquery = jnp.einsum("hsk,kd->hsd", dscores, items[2], preferred_element_type=jnp.float32)
        return (dquery, key_gradient, value_gradient)

    dquery, key_gradient, value_gradient = lax.map(local_grads, stacked + (delta,))
    dquery = dquery.transpose(2, 0, 1, 3).reshape(1, seq_rows, q_heads * HEAD_WIDTH)
    query_grad = lax.psum_scatter(
        dquery.astype(jnp.bfloat16), "trunk", scatter_dimension=1, tiled=True
    )
    key_gradient = key_gradient.transpose(1, 0, 2).reshape(-1, kv_heads * HEAD_WIDTH)
    value_gradient = value_gradient.transpose(1, 0, 2).reshape(-1, kv_heads * HEAD_WIDTH)
    trunk_key_grad, trunk_value_grad = (
        lax.psum_scatter(
            key_gradient[:slab_rows].astype(jnp.bfloat16), "branch", scatter_dimension=0, tiled=True
        ).astype(jnp.float32),
        lax.psum_scatter(
            value_gradient[:slab_rows].astype(jnp.bfloat16),
            "branch",
            scatter_dimension=0,
            tiled=True,
        ).astype(jnp.float32),
    )
    branch_key_grad = key_gradient[slab_rows:][None].astype(jnp.bfloat16)
    branch_value_grad = value_gradient[slab_rows:][None].astype(jnp.bfloat16)
    return (
        query_grad,
        trunk_key_grad.astype(jnp.bfloat16),
        trunk_value_grad.astype(jnp.bfloat16),
        branch_key_grad,
        branch_value_grad,
    )


MESH = pl.DeviceIdType.MESH
W = HEAD_WIDTH
NT = (((1,), (1,)), ((), ()))
TN = (((0,), (0,)), ((), ()))
HIDDEN = -1e30


def dot(lhs, rhs, dims=None):
    if dims is None:
        return jnp.dot(lhs, rhs, preferred_element_type=jnp.float32)
    return lax.dot_general(lhs, rhs, dims, preferred_element_type=jnp.float32)


def fused_kernel(
    forks,
    lengths,
    query,
    cotangent,
    branch_keys,
    branch_values,
    trunk_keys,
    trunk_values,
    query_grad,
    z_in,
    own_in,
    kv_here,
    q_here,
    own_here,
    q_in,
    kv,
    own,
    q_rows,
    c_rows,
    scores,
    dprobs,
    dq_total,
    mine,
    x_out,
    x_in,
    z_out,
    own_out,
    dq_out,
    limits_out,
    limits_in,
    local_sem,
    z_send,
    z_recv,
    x_send,
    x_recv,
    back_send,
    back_recv,
):
    z = lax.axis_index("trunk")
    x = lax.axis_index("branch")
    core = lax.axis_index("tensor")
    head = lax.rem(z, 2)
    at = (z, z + 1 - 2 * head, lax.rem(z + 2, 4), 3 - z)
    workers = [{"trunk": there, "branch": core, "tensor": 1 - x} for there in at]
    homes = [{"trunk": there, "branch": 1 - core, "tensor": x} for there in at]
    twin = {"tensor": 1 - core}
    rows = query.shape[1]
    slab = trunk_keys.shape[0]
    group = query.shape[2] // 2 // W
    wide = group * W
    cols = 2 * group * rows
    scale = W ** (-0.5)

    def head_cols(index, width):
        return pl.ds(pl.multiple_of(index * width, width), width)

    local = []
    for i in (0, 1):
        for n, ref in enumerate((trunk_keys, trunk_values)):
            local.append((ref.at[:, pl.ds(i * W, W)], kv_here.at[i, n]))
        for n, ref in enumerate((query, cotangent)):
            local.append((ref.at[0, :, pl.ds(i * wide, wide)], q_here.at[i, n]))
        for n, ref in enumerate((branch_keys, branch_values)):
            local.append((ref.at[0, :, pl.ds(i * W, W)], own_here.at[i, n]))
    local = [
        pltpu.make_async_copy(src, dst, local_sem.at[k]) for k, (src, dst) in enumerate(local)
    ]
    for copy in local:
        copy.start()
    barrier = pltpu.get_barrier_semaphore()
    for device in workers + homes:
        pl.semaphore_signal(barrier, inc=1, device_id=device, device_id_type=MESH)
    pl.semaphore_wait(barrier, len(workers + homes))

    def remote(src, dst, send, recv, device):
        return pltpu.make_async_remote_copy(
            src_ref=src,
            dst_ref=dst,
            send_sem=send,
            recv_sem=recv,
            device_id=device,
            device_id_type=MESH,
        )

    limits_out[0] = jnp.full(limits_out.shape[1:], forks[0], jnp.int32)
    limits_out[1] = jnp.full(limits_out.shape[1:], lengths[0], jnp.int32)
    z_copies = {}
    for d in range(4):
        sent = lax.rem(at[d], 2)
        z_copies[d] = [
            remote(here.at[sent], there(d), z_send.at[d, n], z_recv.at[d, n], workers[d])
            for n, (here, there) in enumerate(
                (
                    (kv_here, lambda d: kv.at[0, :, d]),
                    (own_here, lambda d: own.at[:, d]),
                    (q_here, lambda d: q_in.at[d]),
                )
            )
            if n < 2 or d < 2
        ]
    limits = remote(limits_out, limits_in, z_send.at[2, 2], z_recv.at[2, 2], workers[0])
    for copy in local:
        copy.wait()
    limits.start()
    for d in (1, 2, 3, 0):
        z_copies[d][0].start()
    for d in (3, 1, 2, 0):
        z_copies[d][1].start()
    for d in (1, 0):
        z_copies[d][2].start()

    x_copies = {}
    for d in (1, 2, 3, 0):
        z_copies[d][0].wait_recv()
        x_copies[d] = remote(kv.at[0, :, d], kv.at[1, :, d], x_send.at[d], x_recv.at[d], twin)
        x_copies[d].start()
    limits.wait_recv()
    for e in (0, 1):
        z_copies[e][2].wait_recv()

    fork = limits_in[0, 0:1, 0:1]
    length = limits_in[1, 0:1, 0:1]
    row_iota = lax.broadcasted_iota(jnp.int32, (rows, W), 0)
    for e in (0, 1):
        live = (row_iota + at[e] * rows < length).astype(jnp.float32)
        for g in range(group):
            start = (e * group + g) * rows
            q_rows[start : start + rows, :] = q_in[e, 0, :, g * W : (g + 1) * W]
            part = q_in[e, 1, :, g * W : (g + 1) * W].astype(jnp.float32) * live
            c_rows[start : start + rows, :] = part.astype(jnp.bfloat16)

    col = lax.broadcasted_iota(jnp.int32, (1, cols), 1)
    half = group * rows
    col_pos = jnp.where(col < half, at[0], at[1]) * rows + lax.rem(col, rows)
    slab_iota = lax.broadcasted_iota(jnp.int32, (slab, 1), 0)

    own_base = 8 * slab
    own_rows = 4 * rows

    def score(base, size, key, value, seen):
        part = dot(key, q_rows[...], NT) * scale
        part = jnp.where(seen, part, HIDDEN)
        scores[base : base + size, :] = part
        dprobs[base : base + size, :] = dot(value, c_rows[...], NT)
        return jnp.max(part, 0, keepdims=True)

    def trunk_score(r):
        side = 1 - core if r == 0 else core
        pos = jnp.concatenate([slab_iota + (there * 2 + side) * slab for there in at], 0)
        key, value = [kv[r, n].reshape(4 * slab, W) for n in (0, 1)]
        return score(r * 4 * slab, 4 * slab, key, value, pos < fork)

    largest = trunk_score(0)
    for d in range(4):
        z_copies[d][1].wait_recv()
    own_iota = lax.broadcasted_iota(jnp.int32, (rows, 1), 0)
    own_pos = jnp.concatenate([own_iota + at[d] * rows for d in range(4)], 0)
    own_key = own[0].reshape(own_rows, W)
    own_value = own[1].reshape(own_rows, W)
    largest = jnp.maximum(
        largest,
        score(
            own_base, own_rows, own_key, own_value, (own_pos <= col_pos) & (own_pos < length)
        ),
    )
    for d in (1, 2, 3, 0):
        x_copies[d].wait_recv()
    largest = jnp.maximum(largest, trunk_score(1))

    total = jnp.zeros((1, cols), jnp.float32)
    delta = jnp.zeros((1, cols), jnp.float32)
    for base in range(0, own_base + own_rows, W):
        weights = jnp.exp(scores[base : base + W, :] - largest)
        scores[base : base + W, :] = weights
        total += jnp.sum(weights, 0, keepdims=True)
        delta += jnp.sum(weights * dprobs[base : base + W, :], 0, keepdims=True)
    inverse = 1.0 / total
    delta = delta * inverse
    dq_total[...] = jnp.zeros_like(dq_total)

    def grads(base, size, key):
        probs = scores[base : base + size, :] * inverse
        low = probs.astype(jnp.bfloat16)
        dscores = (probs * (dprobs[base : base + size, :] - delta) * scale).astype(jnp.bfloat16)
        dq_total[...] += dot(key, dscores, TN)
        return dot(dscores, q_rows[...]), dot(low, c_rows[...])

    back = {}
    pair = grads(own_base, own_rows, own_key)
    for n in (0, 1):
        mine_part = pair[n].astype(jnp.bfloat16)
        for d in range(4):
            own_out[d, n] = mine_part[d * rows : (d + 1) * rows, :]
    for d in (3, 1, 2, 0):
        back[4 + d] = remote(
            own_out.at[d], own_in.at[d], back_send.at[4 + d], back_recv.at[4 + d], homes[d]
        )
        back[4 + d].start()
    for d in (3, 2, 1, 0):
        if d in (3, 1):
            key = kv[1, 0, d - 1 : d + 1].reshape(2 * slab, W)
            pair = grads((3 + d) * slab, 2 * slab, key)
        for n in (0, 1):
            part = pair[n][d % 2 * slab : (d % 2 + 1) * slab]
            x_out[d, n] = part.astype(jnp.bfloat16)
        back[d] = remote(x_out.at[d], x_in.at[d], back_send.at[d], back_recv.at[d], twin)
        back[d].start()
    pair = grads(0, 4 * slab, kv[0, 0].reshape(4 * slab, W))
    for d in range(4):
        for n in (0, 1):
            mine[d, n] = pair[n][d * slab : (d + 1) * slab]
    dq = dq_total[...].T.astype(jnp.bfloat16)
    for e in (1, 0):
        for g in range(group):
            start = e * half + g * rows
            dq_out[e, :, g * W : (g + 1) * W] = dq[start : start + rows, :]
    for e in (1, 0):
        back[12 + e] = remote(
            dq_out.at[e],
            query_grad.at[0, :, head_cols(head, wide)],
            back_send.at[12 + e],
            back_recv.at[12 + e],
            homes[e],
        )
        back[12 + e].start()
    for d in (3, 1, 2, 0):
        back[d].wait_recv()
        z_out[d] = (mine[d] + x_in[d].astype(jnp.float32)).astype(jnp.bfloat16)
        back[8 + d] = remote(
            z_out.at[d], z_in.at[d], back_send.at[8 + d], back_recv.at[8 + d], homes[d]
        )
        back[8 + d].start()
    for key, copy in back.items():
        if key >= 4:
            copy.wait_recv()
    limits.wait_send()
    for copy in sum(z_copies.values(), []):
        copy.wait_send()
    for copies in (x_copies, back):
        for copy in copies.values():
            copy.wait_send()


def owners_sum(
    query_in,
    z_in,
    own_in,
    query_grad,
    trunk_key_grad,
    trunk_value_grad,
    branch_key_grad,
    branch_value_grad,
    dq,
    shares,
    own_shares,
    slabs,
    branches,
    sems,
):
    head = lax.rem(lax.axis_index("trunk"), 2)
    f32 = jnp.float32
    arrive = [
        pltpu.make_async_copy(src, dst, sems.at[n])
        for n, (src, dst) in enumerate(((query_in, dq), (z_in, shares), (own_in, own_shares)))
    ]
    results = (
        (dq, query_grad),
        (slabs.at[0], trunk_key_grad),
        (slabs.at[1], trunk_value_grad),
        (branches.at[0], branch_key_grad.at[0]),
        (branches.at[1], branch_value_grad.at[0]),
    )
    leave = [
        pltpu.make_async_copy(src, dst, sems.at[3 + n]) for n, (src, dst) in enumerate(results)
    ]

    def add(total, parts):
        for a, b, which in ((0, 2, head), (1, 3, 1 - head)):
            at = pl.ds(pl.multiple_of(which * W, W), W)
            for n in (0, 1):
                both = parts[a, n].astype(f32) + parts[b, n].astype(f32)
                total[n, :, at] = both.astype(jnp.bfloat16)

    for copy in arrive:
        copy.start()
    arrive[0].wait()
    leave[0].start()
    arrive[1].wait()
    add(slabs, shares)
    leave[1].start()
    leave[2].start()
    arrive[2].wait()
    add(branches, own_shares)
    leave[3].start()
    leave[4].start()
    for copy in leave:
        copy.wait()


def fused(
    query,
    cotangent,
    branch_keys,
    rollout_value_rows,
    trunk_keys,
    shared_trunk_values,
    forks,
    lengths,
):
    rows = query.shape[1]
    slab = trunk_keys.shape[0]
    wide = query.shape[2] // 2
    cols = 2 * rows * (wide // W)
    keys = 8 * slab + 4 * rows
    bf16, f32 = jnp.bfloat16, jnp.float32
    smem = pl.BlockSpec(memory_space=pltpu.SMEM)
    anywhere = pl.BlockSpec(memory_space=pl.ANY)

    def like(a):
        return jax.ShapeDtypeStruct(a.shape, a.dtype)

    dma = pltpu.SemaphoreType.DMA
    shares = pl.pallas_call(
        fused_kernel,
        out_shape=(
            like(query),
            jax.ShapeDtypeStruct((4, 2, slab, W), bf16),
            jax.ShapeDtypeStruct((4, 2, rows, W), bf16),
        ),
        in_specs=[smem] * 2 + [anywhere] * 6,
        out_specs=(anywhere,) * 3,
        scratch_shapes=[
            pltpu.VMEM((2, 2, slab, W), bf16),
            pltpu.VMEM((2, 2, rows, wide), bf16),
            pltpu.VMEM((2, 2, rows, W), bf16),
            pltpu.VMEM((2, 2, rows, wide), bf16),
            pltpu.VMEM((2, 2, 4, slab, W), bf16),
            pltpu.VMEM((2, 4, rows, W), bf16),
            pltpu.VMEM((cols, W), bf16),
            pltpu.VMEM((cols, W), bf16),
            pltpu.VMEM((keys, cols), f32),
            pltpu.VMEM((keys, cols), f32),
            pltpu.VMEM((W, cols), f32),
            pltpu.VMEM((4, 2, slab, W), f32),
            pltpu.VMEM((4, 2, slab, W), bf16),
            pltpu.VMEM((4, 2, slab, W), bf16),
            pltpu.VMEM((4, 2, slab, W), bf16),
            pltpu.VMEM((4, 2, rows, W), bf16),
            pltpu.VMEM((2, rows, wide), bf16),
            pltpu.VMEM((2, 8, W), jnp.int32),
            pltpu.VMEM((2, 8, W), jnp.int32),
            dma((12,)),
            dma((4, 3)),
            dma((4, 3)),
            dma((4,)),
            dma((4,)),
            dma((14,)),
            dma((14,)),
        ],
        compiler_params=pltpu.CompilerParams(
            collective_id=0, has_side_effects=True, vmem_limit_bytes=60 * 1024 * 1024
        ),
        cost_estimate=pl.CostEstimate(
            flops=10 * keys * cols * W, bytes_accessed=2**20, transcendentals=keys * cols
        ),
    )(
        forks,
        lengths,
        query,
        cotangent,
        branch_keys,
        rollout_value_rows,
        trunk_keys,
        shared_trunk_values,
    )
    return pl.pallas_call(
        owners_sum,
        out_shape=tuple(
            like(a) for a in (query, trunk_keys, shared_trunk_values, branch_keys, rollout_value_rows)
        ),
        in_specs=[anywhere] * 3,
        out_specs=(anywhere,) * 5,
        scratch_shapes=[
            pltpu.VMEM(query.shape, bf16),
            pltpu.VMEM((4, 2, slab, W), bf16),
            pltpu.VMEM((4, 2, rows, W), bf16),
            pltpu.VMEM((2, slab, 2 * W), bf16),
            pltpu.VMEM((2, rows, 2 * W), bf16),
            dma((8,)),
        ],
        compiler_params=pltpu.CompilerParams(vmem_limit_bytes=60 * 1024 * 1024),
    )(*shares)


def plan_of(mesh):
    if mesh.shape["trunk"] == 4 and mesh.shape["branch"] == 2 and mesh.shape["tensor"] == 2:
        return fused
    return shards


def solution(mesh):
    return jax.shard_map(
        plan_of(mesh),
        mesh=mesh,
        in_specs=(
            P(("groups", "branch"), "trunk", "tensor"),
            P(("groups", "branch"), "trunk", "tensor"),
            P(("groups", "branch"), "trunk", "tensor"),
            P(("groups", "branch"), "trunk", "tensor"),
            P(("groups", "trunk", "branch"), "tensor"),
            P(("groups", "trunk", "branch"), "tensor"),
            P(("groups", "branch")),
            P(("groups", "branch")),
        ),
        out_specs=(
            P(("groups", "branch"), "trunk", "tensor"),
            P(("groups", "trunk", "branch"), "tensor"),
            P(("groups", "trunk", "branch"), "tensor"),
            P(("groups", "branch"), "trunk", "tensor"),
            P(("groups", "branch"), "trunk", "tensor"),
        ),
        check_vma=False,
    )
```
